128 devices in a mesh: row: 8 (over z, y_lo), col: 16 (over x, y_hi, core).
Axes of the slice: x: 4, y: 4 (y_hi: 2, y_lo: 2; y = y_hi * 2 + y_lo), z: 4, core: 2. Of those that a mesh axis runs over, the one named last changes fastest.
Arguments:
- picture: bfloat16 [64, 256, 8192], P(None, 'row', 'col'), may hold values from -6 to 6
- input_gain: float32 [64], replicated, may hold values from 0.5 to 1.5
- input_weight: bfloat16 [64, 128], replicated, may hold values from -0.75 to 0.75
- grid_branch_scale: float32 [64], replicated, may hold values from 0.5 to 1.5
- grid_widen_weight: bfloat16 [64, 128], replicated, may hold values from -0.75 to 0.75
- grid_gate_scale: float32 [64], replicated, may hold values from 0.5 to 1.5
- grid_mixing: bfloat16 [256, 256], replicated, may hold values from -0.375 to 0.375
- grid_bias: float32 [256], replicated, may hold values from -4 to 4
- grid_narrow_weight: bfloat16 [64, 64], replicated, may hold values from -0.75 to 0.75
- block_branch_scale: float32 [64], replicated, may hold values from 0.5 to 1.5
- block_widen_weight: bfloat16 [64, 128], replicated, may hold values from -0.75 to 0.75
- block_gate_scale: float32 [64], replicated, may hold values from 0.5 to 1.5
- block_mixing: bfloat16 [256, 256], replicated, may hold values from -0.375 to 0.375
- block_bias: float32 [256], replicated, may hold values from -4 to 4
- block_narrow_weight: bfloat16 [64, 64], replicated, may hold values from -0.75 to 0.75
- output_weight: bfloat16 [128, 64], replicated, may hold values from -0.5 to 0.5
Outputs:
- refined: bfloat16 [64, 256, 8192], P(None, 'row', 'col')
The draws below stay inside these ranges and needn't reach their ends.
All inputs are finite; a program needn't handle non-finite values.
Results may differ from the reference program's by a relative error of at most 0.01.
Values may be sent and summed in bfloat16 or wider, within the bound.
No kernel may reach another device: no remote copies, remote signals or barrier semaphores. Data moves between devices by JAX's collectives and lax.ppermute only.
A program may use at most 128 MiB of HBM per device.

```python
import jax
import jax.numpy as jnp
from jax import lax

C = 64
HID = 128
GRID_SIDE = 16
BLOCK_SIDE = 16
GRID = 256
BLOCK = 256
H = 256
W = 8192


def block_scale(rng, extent, cuts, least, largest):
    level = 1.0
    for position, blocks in cuts:
        heights = jax.random.uniform(jax.random.fold_in(jax.random.fold_in(rng, 6), position), (blocks,), jnp.float32, least / len(cuts), largest / len(cuts))
        level = level * jnp.repeat(jnp.exp(heights), extent[position] // blocks).reshape((-1,) + (1,) * (len(extent) - 1 - position))
    return level


def bell_draw(key, shape, scale, most, cuts=(), kind=jnp.bfloat16):
    array = jax.random.normal(key, shape, jnp.float32) * scale
    if len(cuts) > 0:
        array = block_scale(key, shape, cuts, -0.22, 0.18) * array
    return jnp.clip(array, min=-most, max=most).astype(kind)


def setup_inputs(seed: int = 0) -> dict:
    arg_keys = jax.random.split(jax.random.key(seed), 17)
    return {
        "picture": bell_draw(arg_keys[0], (C, H, W), 1.0, 6.0, ((1, 8), (2, 16))),
        "input_gain": jnp.clip(1.0 + 0.1 * jax.random.normal(arg_keys[1], (C,), jnp.float32), 0.5, 1.5),
        "input_weight": bell_draw(arg_keys[2], (C, HID), C ** -0.5, 0.75),
        "grid_branch_scale": jnp.clip(1.0 + 0.1 * jax.random.normal(arg_keys[3], (C,), jnp.float32), 0.5, 1.5),
        "grid_widen_weight": bell_draw(arg_keys[4], (C, HID), C ** -0.5, 0.75),
        "grid_gate_scale": jnp.clip(1.0 + 0.1 * jax.random.normal(arg_keys[5], (C,), jnp.float32), 0.5, 1.5),
        "grid_mixing": bell_draw(arg_keys[6], (GRID, GRID), GRID ** -0.5, 0.375),
        "grid_bias": bell_draw(arg_keys[7], (GRID,), 1.0, 4.0, (), jnp.float32),
        "grid_narrow_weight": bell_draw(arg_keys[8], (C, C), C ** -0.5, 0.75),
        "block_branch_scale": jnp.clip(1.0 + 0.1 * jax.random.normal(arg_keys[9], (C,), jnp.float32), 0.5, 1.5),
        "block_widen_weight": bell_draw(arg_keys[10], (C, HID), C ** -0.5, 0.75),
        "block_gate_scale": jnp.clip(1.0 + 0.1 * jax.random.normal(arg_keys[11], (C,), jnp.float32), 0.5, 1.5),
        "block_mixing": bell_draw(arg_keys[12], (BLOCK, BLOCK), BLOCK ** -0.5, 0.375),
        "block_bias": bell_draw(arg_keys[13], (BLOCK,), 1.0, 4.0, (), jnp.float32),
        "block_narrow_weight": bell_draw(arg_keys[14], (C, C), C ** -0.5, 0.75),
        "output_weight": bell_draw(arg_keys[15], (HID, C), HID ** -0.5, 0.5),
    }


EPSILON = 1e-06

def layer_norm(values, scale_gain):
    values = values.astype(jnp.float32)
    center = values - lax.optimization_barrier(jnp.mean(values, axis=-1, keepdims=True))
    spread = lax.optimization_barrier(jnp.mean(center * center, axis=-1, keepdims=True))
    return center * lax.rsqrt(spread + EPSILON) * scale_gain

def project(values, weight):
    flattened = values.reshape(-1, values.shape[-1])
    product = jnp.dot(flattened, weight, preferred_element_type=jnp.float32)
    return product.reshape(values.shape[:-1] + (weight.shape[1],))

def input_section(strip, input_gain, input_weight):
    pixels = jnp.transpose(strip, (1, 2, 0))
    normed = layer_norm(pixels, input_gain).astype(jnp.bfloat16)
    return jax.nn.gelu(project(normed, input_weight)).astype(jnp.bfloat16)

def branch_former(branch_input_tensor, scale_gain, expand_weight, gate_gain):
    normed = layer_norm(branch_input_tensor, scale_gain).astype(jnp.bfloat16)
    expanded = jax.nn.gelu(project(normed, expand_weight)).astype(jnp.bfloat16)
    half_width = expanded.shape[-1] // 2
    gate_input_tensor = layer_norm(expanded[..., half_width:], gate_gain).astype(jnp.bfloat16)
    return (expanded[..., :half_width], gate_input_tensor)

def branch_latter(branch_input_tensor, passthrough, blended, narrow_weight):
    gated_value_rows = (passthrough.astype(jnp.float32) * (blended.astype(jnp.float32) + 1.0)).astype(jnp.bfloat16)
    return (branch_input_tensor.astype(jnp.float32) + project(gated_value_rows, narrow_weight)).astype(jnp.bfloat16)

def block_gating(gate_input_tensor, mixing, offset_bias):
    row_total, col_total, channels = gate_input_tensor.shape
    blocked = gate_input_tensor.reshape(row_total // BLOCK_SIDE, BLOCK_SIDE, col_total // BLOCK_SIDE, BLOCK_SIDE, channels)
    weights = mixing.astype(jnp.float32).reshape(BLOCK_SIDE, BLOCK_SIDE, BLOCK_SIDE, BLOCK_SIDE)
    result = jnp.einsum('ipjqc,pqPQ->iPjQc', blocked.astype(jnp.float32), weights)
    result = result + offset_bias.reshape(1, BLOCK_SIDE, 1, BLOCK_SIDE, 1)
    return result.astype(jnp.bfloat16).reshape(row_total, col_total, channels)

def reference(picture, input_gain, input_weight, grid_branch_scale, grid_widen_weight, grid_gate_scale, grid_mixing, grid_bias, grid_narrow_weight, block_branch_scale, block_widen_weight, block_gate_scale, block_mixing, block_bias, block_narrow_weight, output_weight):
    strips = H // BLOCK_SIDE
    row_stride = H // GRID_SIDE
    col_stride = W // GRID_SIDE

    def take_strip(strip_index):
        return lax.dynamic_slice_in_dim(picture, strip_index * BLOCK_SIDE, BLOCK_SIDE, 1)

    def gate_input(strip_index):
        hidden = input_section(take_strip(strip_index), input_gain, input_weight)
        return branch_former(hidden[..., :C], grid_branch_scale, grid_widen_weight, grid_gate_scale)[1]
    gate_all = lax.map(gate_input, jnp.arange(strips, dtype=jnp.int32)).reshape(H, W, C)
    gate_cells = gate_all.reshape(GRID_SIDE, row_stride, GRID_SIDE, col_stride, C)
    mixing_table = grid_mixing.astype(jnp.float32).reshape(GRID_SIDE, GRID_SIDE, GRID_SIDE, GRID_SIDE)

    def mix_offset(offset):
        layer_slice = lax.dynamic_index_in_dim(gate_cells, offset, 1, keepdims=False)
        product = jnp.einsum('ijbc,ijIJ->IJbc', layer_slice.astype(jnp.float32), mixing_table)
        product = product + grid_bias.reshape(GRID_SIDE, GRID_SIDE, 1, 1)
        return product.astype(jnp.bfloat16)
    stacked = lax.map(mix_offset, jnp.arange(row_stride, dtype=jnp.int32))
    mixed_all = jnp.transpose(stacked, (1, 0, 2, 3, 4)).reshape(H, W, C)

    def finish(strip_index):
        strip = take_strip(strip_index)
        hidden = input_section(strip, input_gain, input_weight)
        grid_input_tensor = hidden[..., :C]
        block_input_tensor = hidden[..., C:]
        passthrough = branch_former(grid_input_tensor, grid_branch_scale, grid_widen_weight, grid_gate_scale)[0]
        grid_blended = lax.dynamic_slice_in_dim(mixed_all, strip_index * BLOCK_SIDE, BLOCK_SIDE, 0)
        grid_output_tensor = branch_latter(grid_input_tensor, passthrough, grid_blended, grid_narrow_weight)
        block_passthrough, block_gate_tensor = branch_former(block_input_tensor, block_branch_scale, block_widen_weight, block_gate_scale)
        block_blended = block_gating(block_gate_tensor, block_mixing, block_bias)
        block_output_tensor = branch_latter(block_input_tensor, block_passthrough, block_blended, block_narrow_weight)
        joined = jnp.concatenate([grid_output_tensor, block_output_tensor], axis=-1)
        pixels = jnp.transpose(strip, (1, 2, 0)).astype(jnp.float32)
        result = (pixels + project(joined, output_weight)).astype(jnp.bfloat16)
        return jnp.transpose(result, (2, 0, 1))
    pieces = lax.map(finish, jnp.arange(strips, dtype=jnp.int32))
    return jnp.transpose(pieces, (1, 0, 2, 3)).reshape(C, H, W)
```

```python
import jax
import jax.numpy as jnp
from jax import lax
from jax.experimental import pallas as pl
from jax.experimental.pallas import tpu as pltpu
from jax.sharding import PartitionSpec as P

F32 = jnp.float32
BF16 = jnp.bfloat16
C = 64
SIDE = 16
CELLS = 256
LANES = 128
COLS = 512
QUARTERS = COLS // LANES
TILES = 2 * QUARTERS
STRIP = SIDE * LANES
PEERS = 128
HALF = C // 2
EPSILON = 1e-06
GELU_A = 0.7978845608
GELU_B = 0.7978845608 * 0.044715


def mm(a, b):
    return jnp.dot(a, b, preferred_element_type=F32)


def short(value):
    return jnp.array(value, BF16)


def averages(values):
    return mm(jnp.full((16, C), 1.0 / C, BF16), values)


def center(values):
    n = values.shape[1]
    mean = averages(values)
    high = mean.astype(BF16)
    low = (mean - high.astype(F32)).astype(BF16)
    centered = (values.reshape(C // 16, 16, n) - high[None]) - low[None]
    centered = centered.reshape(C, n)
    scale = lax.rsqrt(averages(centered * centered) + EPSILON)
    return centered, scale


def rescale(values, scale):
    rows, n = values.shape
    return (values.reshape(rows // 16, 16, n) * scale[None]).reshape(rows, n)


def gelu(values):
    v = values.astype(BF16)
    bend = jnp.tanh(v * (v * v * short(GELU_B) + short(GELU_A)))
    half = v * short(0.5)
    return half * bend + half


def widen(values, weight):
    centered, scale = center(values)
    return gelu(rescale(mm(weight, centered), scale))


def whiten(values):
    centered, scale = center(values)
    return rescale(centered, scale.astype(BF16))


def gained(weight, gain):
    return (weight.astype(F32).T * gain).astype(BF16)


def strip_of(picture, tile):
    cell = tile // QUARTERS
    quarter = tile % QUARTERS
    values = picture[
        :,
        pl.ds(pl.multiple_of(cell * SIDE, SIDE), SIDE),
        pl.ds(pl.multiple_of(quarter * LANES, LANES), LANES),
    ]
    values = pltpu.einshape("crl->rcl", values)
    return jnp.concatenate([values[r] for r in range(SIDE)], axis=1)


def gate_kernel(picture, in_gain, in_weight, wide_gain, wide_weight, gate, held):
    first = gained(in_weight[...], in_gain[...])[:C]
    second = gained(wide_weight[...], wide_gain[...])[C:]

    def body(tile, carry):
        cell = tile // QUARTERS
        quarter = tile % QUARTERS
        values = strip_of(picture, tile)
        hidden = widen(values, first)
        features = whiten(widen(hidden, second))
        for a in range(SIDE):
            for part in range(2):
                peer = a * (2 * QUARTERS) + quarter * 2 + part
                gate[peer, pl.ds(pl.multiple_of(cell * HALF, HALF), HALF), :] = features[
                    part * HALF : (part + 1) * HALF, a * LANES : (a + 1) * LANES
                ]
        held[tile] = hidden
        return carry

    lax.fori_loop(0, TILES, body, 0)


def local_kernel(
    picture, hidden_in, bias_pair,
    in_gain, in_weight,
    grid_gain, grid_wide, grid_gate_gain, grid_mixing, grid_narrow,
    block_gain, block_wide, block_gate_gain, block_mixing, block_bias, block_narrow,
    out_weight,
    passed, base, final_weight, mixing_out,
    spread, keys, kept, mixed,
):
    wide = SIDE * LANES
    source = lax.broadcasted_iota(jnp.int32, (CELLS, wide), 0)
    target = lax.broadcasted_iota(jnp.int32, (CELLS, wide), 1)
    chosen = (target // LANES) * SIDE + target % SIDE
    pick = jnp.where(source == chosen, 1.0, 0.0).astype(BF16)
    expanded = mm(block_mixing[...], pick).astype(BF16)
    same = lax.broadcasted_iota(jnp.int32, (LANES, wide), 0) // SIDE == (
        lax.broadcasted_iota(jnp.int32, (LANES, wide), 1) % LANES
    ) // SIDE
    mask = jnp.where(same, 1.0, 0.0).astype(BF16)
    for p in range(SIDE):
        rows = expanded[p * SIDE : (p + 1) * SIDE]
        rows = jnp.concatenate([rows] * (LANES // SIDE), axis=0)
        spread[p * LANES : (p + 1) * LANES, :] = rows * mask
    offset = mm(block_bias[...].astype(BF16), pick)
    rest = block_bias[...] - block_bias[...].astype(BF16).astype(F32)
    offset = offset + mm(rest.astype(BF16), pick)
    offset = (offset[:1] + 1.0).astype(BF16)

    place = lax.broadcasted_iota(jnp.int32, (CELLS, CELLS), 0)
    cell = lax.broadcasted_iota(jnp.int32, (CELLS, CELLS), 1)
    wanted = ((place // 32) * 2 + place % 2) * SIDE + (place // 2) % SIDE
    order = jnp.where(cell == wanted, 1.0, 0.0).astype(BF16)
    last = (((1,), (1,)), ((), ()))
    turned = lax.dot_general(order, grid_mixing[...], last, preferred_element_type=F32).astype(BF16)
    mixing_out[...] = lax.dot_general(turned, order, last, preferred_element_type=F32).astype(BF16)

    out_turned = out_weight[...].astype(F32).T.astype(BF16)
    over = (((1,), (1,)), ((), ()))
    grid_both = lax.dot_general(out_turned[:, :C], grid_narrow[...], over, preferred_element_type=F32)
    block_both = lax.dot_general(out_turned[:, C:], block_narrow[...], over, preferred_element_type=F32)
    final_weight[...] = (grid_both * grid_gate_gain[...]).astype(BF16)
    block_gained = (block_both * block_gate_gain[...]).astype(BF16)
    block_plain = block_both.astype(BF16)

    first = gained(in_weight[...], in_gain[...])[C:]
    grid_second = gained(grid_wide[...], grid_gain[...])[:C]
    block_second = gained(block_wide[...], block_gain[...])

    def before(tile, carry):
        values = strip_of(picture, tile)
        grid_hidden = hidden_in[tile]
        block_hidden = widen(values, first)
        grid_pass = widen(grid_hidden, grid_second)
        passed[tile] = grid_pass
        both = widen(block_hidden, block_second)
        kept[tile] = both[:C]
        rows = pl.ds(pl.multiple_of(tile * C, C), C)
        keys[rows, :] = whiten(both[C:])
        weight = (grid_both * (bias_pair[0, tile // QUARTERS] + 1.0)).astype(BF16)
        total = mm(out_turned, jnp.concatenate([grid_hidden, block_hidden], axis=0))
        total = total + mm(weight, grid_pass)
        base[tile] = values.astype(F32) + total
        return carry

    lax.fori_loop(0, TILES, before, 0)

    def mix(step, carry):
        columns = pl.ds(pl.multiple_of(step * CELLS, CELLS), CELLS)
        mixed[:, columns] = mm(keys[...], spread[:, columns]).astype(BF16)
        return carry

    lax.fori_loop(0, wide // CELLS, mix, 0)

    def after(tile, carry):
        rows = pl.ds(pl.multiple_of(tile * C, C), C)
        through = kept[tile]
        total = mm(block_gained, through * mixed[rows, :]) + mm(block_plain, through * offset)
        base[tile] = base[tile] + total
        return carry

    lax.fori_loop(0, TILES, after, 0)


def mix_kernel(arrived, mixing, sent, wide_in, wide_out):
    groups = 16
    span = PEERS // groups

    def unpack(step, carry):
        part = arrived[pl.ds(step * span, span)].astype(F32)
        rows = span * C
        wide_in[pl.ds(pl.multiple_of(step * rows, rows), rows), :] = part.reshape(rows, LANES)
        return carry

    lax.fori_loop(0, groups, unpack, 0)
    weight = mixing[...]

    def mix(step, carry):
        pair = []
        for k in range(2):
            rows = pl.ds(step * 2 + k, CELLS, stride=HALF)
            pair.append(wide_in[rows, :].astype(BF16))
        result = mm(weight, jnp.concatenate(pair, axis=1))
        for k in range(2):
            rows = pl.ds(step * 2 + k, CELLS, stride=HALF)
            wide_out[rows, :] = result[:, k * LANES : (k + 1) * LANES]
        return carry

    lax.fori_loop(0, HALF // 2, mix, 0)

    def pack(step, carry):
        rows = span * C
        part = wide_out[pl.ds(pl.multiple_of(step * rows, rows), rows), :].astype(BF16)
        sent[pl.ds(step * span, span)] = part.reshape(span, C, LANES)
        return carry

    lax.fori_loop(0, groups, pack, 0)


def final_kernel(returned, passed, base, weight, refined):
    final = weight[...]

    def body(tile, carry):
        cell = tile // QUARTERS
        quarter = tile % QUARTERS
        rows = pl.ds(pl.multiple_of(cell * HALF, HALF), HALF)
        pieces = []
        for a in range(SIDE):
            peer = a * (2 * QUARTERS) + quarter * 2
            pieces.append(
                jnp.concatenate([returned[peer, rows, :], returned[peer + 1, rows, :]], axis=0)
            )
        mixed = jnp.concatenate(pieces, axis=1)
        total = (base[tile] + mm(final, passed[tile] * mixed)).astype(BF16)
        total = jnp.stack([total[:, a * LANES : (a + 1) * LANES] for a in range(SIDE)])
        refined[
            :,
            pl.ds(pl.multiple_of(cell * SIDE, SIDE), SIDE),
            pl.ds(pl.multiple_of(quarter * LANES, LANES), LANES),
        ] = pltpu.einshape("rcl->crl", total)
        return carry

    lax.fori_loop(0, TILES, body, 0)


def kernel_call(kernel, name, outputs, scratch, limit, flops, *operands, smem=()):
    whole = pl.BlockSpec(memory_space=pltpu.VMEM)
    scalars = pl.BlockSpec(memory_space=pltpu.SMEM)
    return pl.pallas_call(
        kernel,
        in_specs=[scalars if i in smem else whole for i in range(len(operands))],
        out_specs=[whole] * len(outputs),
        out_shape=[jax.ShapeDtypeStruct(s, t) for s, t in outputs],
        scratch_shapes=scratch,
        name=name,
        cost_estimate=pl.CostEstimate(flops=flops, bytes_accessed=1 << 22, transcendentals=0),
        compiler_params=pltpu.CompilerParams(vmem_limit_bytes=limit << 20),
    )(*operands)


def exchange(values):
    return lax.all_to_all(values, ("row", "col"), split_axis=0, concat_axis=0, tiled=True)


def on_device(
    picture,
    input_gain,
    input_weight,
    grid_branch_scale,
    grid_widen_weight,
    grid_gate_scale,
    grid_mixing,
    grid_bias,
    grid_narrow_weight,
    block_branch_scale,
    block_widen_weight,
    block_gate_scale,
    block_mixing,
    block_bias,
    block_narrow_weight,
    output_weight,
):
    row = lambda gain: gain.reshape(1, -1)
    pieces = ((PEERS, C, LANES), BF16)
    tiles = (TILES, C, STRIP)
    gate, hidden = kernel_call(
        gate_kernel, "gate", [pieces, (tiles, BF16)], [], 24, 1 << 30,
        picture, row(input_gain), input_weight, row(grid_branch_scale), grid_widen_weight,
    )
    arrived = exchange(gate)
    position = lax.axis_index("row") * 2 * SIDE + lax.axis_index("col")
    own_bias = jnp.stack(
        [
            lax.dynamic_index_in_dim(grid_bias, position, keepdims=False),
            lax.dynamic_index_in_dim(grid_bias, position + SIDE, keepdims=False),
        ]
    ).reshape(1, 2)
    passed, base, final_weight, mixing = kernel_call(
        local_kernel, "local",
        [(tiles, BF16), (tiles, F32), ((C, C), BF16), ((CELLS, CELLS), BF16)],
        [
            pltpu.VMEM((STRIP, STRIP), BF16),
            pltpu.VMEM((TILES * C, STRIP), BF16),
            pltpu.VMEM(tiles, BF16),
            pltpu.VMEM((TILES * C, STRIP), BF16),
        ],
        34, 20 << 30,
        picture, hidden, own_bias,
        row(input_gain), input_weight,
        row(grid_branch_scale), grid_widen_weight, row(grid_gate_scale), grid_mixing,
        grid_narrow_weight,
        row(block_branch_scale), block_widen_weight, row(block_gate_scale), block_mixing,
        row(block_bias), block_narrow_weight,
        output_weight,
        smem=(2,),
    )
    rows = PEERS * C
    (sent,) = kernel_call(
        mix_kernel, "mix", [pieces],
        [pltpu.VMEM((rows, LANES), F32), pltpu.VMEM((rows, LANES), F32)],
        24, 1 << 30, arrived, mixing,
    )
    returned = exchange(sent)
    (refined,) = kernel_call(
        final_kernel, "final", [(picture.shape, BF16)], [], 24, 1 << 30,
        returned, passed, base, final_weight,
    )
    return refined


def solution(mesh):
    return jax.shard_map(
        on_device,
        mesh=mesh,
        in_specs=(P(None, "row", "col"),) + (P(),) * 15,
        out_specs=P(None, "row", "col"),
        check_vma=False,
    )
```

```python
import jax
import jax.numpy as jnp
from jax import lax
from jax.experimental import pallas as pl
from jax.experimental.pallas import tpu as pltpu
from jax.sharding import PartitionSpec as P

F32 = jnp.float32
BF16 = jnp.bfloat16
C = 64
SIDE = 16
CELLS = 256
LANES = 128
COLS = 512
QUARTERS = COLS // LANES
TILES = 2 * QUARTERS
STRIP = SIDE * LANES
PEERS = 128
PAIR = 2
HALF = C // 2
GROUPS = 4
DEEP = GROUPS * C
WIDE = STRIP // GROUPS
EPSILON = 1e-06
GELU_A = 0.7978845608
GELU_B = 0.7978845608 * 0.044715


def mm(a, b):
    return jnp.dot(a, b, preferred_element_type=F32)


def mm_nt(a, b):
    return lax.dot_general(a, b, (((1,), (1,)), ((), ())), preferred_element_type=F32)


def short(value):
    return jnp.array(value, BF16)


def normalize(values, gain=None):
    n = values.shape[1]
    values = values.astype(F32).reshape(GROUPS, C, n)
    centered = values - jnp.sum(values, axis=1, keepdims=True) * (1.0 / C)
    spread = jnp.sum(centered * centered, axis=1, keepdims=True) * (1.0 / C)
    centered = centered * lax.rsqrt(spread + EPSILON)
    if gain is not None:
        centered = centered * gain[None]
    return centered.astype(BF16).reshape(DEEP, n)


def gelu(values):
    bend = jnp.tanh(values * (GELU_B * (values * values) + GELU_A))
    half = 0.5 * values
    return (half * bend + half).astype(BF16)


def gelu_short(values):
    v = values.astype(BF16)
    bend = jnp.tanh(v * (v * v * short(GELU_B) + short(GELU_A)))
    half = v * short(0.5)
    return half * bend + half


def fourfold(weight):
    wide = jnp.concatenate([weight.astype(BF16)] * GROUPS, axis=1)
    wide = jnp.concatenate([wide] * GROUPS, axis=0)
    rows = lax.broadcasted_iota(jnp.int32, (DEEP, DEEP), 0) // C
    columns = lax.broadcasted_iota(jnp.int32, (DEEP, DEEP), 1) // C
    return wide * jnp.where(rows == columns, 1.0, 0.0).astype(BF16)


def on_rows(gain):
    block = jnp.broadcast_to(gain, (LANES, C)).T
    return jnp.concatenate([block] * (WIDE // LANES), axis=1)


def place_of(tile):
    rows = pl.ds(pl.multiple_of(tile // QUARTERS * SIDE, SIDE), SIDE)
    lanes = pl.ds(pl.multiple_of(tile % QUARTERS * LANES, LANES), LANES)
    return slice(None), rows, lanes


def stack(rows):
    step = SIDE // GROUPS
    groups = [
        jnp.concatenate([rows[g * step + j] for j in range(step)], axis=1) for g in range(GROUPS)
    ]
    return jnp.concatenate(groups, axis=0)


def row_of(values, r):
    step = SIDE // GROUPS
    g, j = r // step, r % step
    return values[g * C : (g + 1) * C, j * LANES : (j + 1) * LANES]


def pixels(block):
    return stack(pltpu.einshape("crl->rcl", block))


def fetch_tiles(picture, held, arrivals):
    copies = [
        pltpu.make_async_copy(picture.at[place_of(t)], held.at[t], arrivals.at[t])
        for t in range(TILES)
    ]
    for copy in copies:
        copy.start()


def wait_tile(picture, held, arrivals, tile):
    pltpu.make_async_copy(picture.at[place_of(tile)], held.at[tile], arrivals.at[tile]).wait()


def gate_place(gate, tile):
    cell, quarter = tile // QUARTERS, tile % QUARTERS
    return gate.at[:, quarter, :, pl.ds(pl.multiple_of(cell * HALF, HALF), HALF), :]


def gate_kernel(
    picture, in_gain, in_weight, wide_gain, wide_weight,
    gate,
    held, made, gains, weights, arrivals, departures, small,
):
    parts = [
        pltpu.make_async_copy(in_weight, weights.at[0], small.at[0]),
        pltpu.make_async_copy(wide_weight, weights.at[1], small.at[1]),
        pltpu.make_async_copy(in_gain, gains.at[0], small.at[2]),
        pltpu.make_async_copy(wide_gain, gains.at[1], small.at[3]),
    ]
    for copy in parts:
        copy.start()
    fetch_tiles(picture, held, arrivals)
    for copy in parts:
        copy.wait()
    first = fourfold(weights[0].astype(F32).T[:C] * gains[0])
    second = fourfold(weights[1].astype(F32).T[C:] * gains[1])

    def body(step, carry):
        tiles = [step * PAIR + k for k in range(PAIR)]
        for tile in tiles:
            wait_tile(picture, held, arrivals, tile)
        values = [normalize(pixels(held[tile])) for tile in tiles]
        values = [gelu_short(mm(first, v)) for v in values]
        values = [normalize(v) for v in values]
        values = [gelu_short(mm(second, v)) for v in values]
        values = [normalize(v) for v in values]
        for tile, features in zip(tiles, values):
            for a in range(SIDE):
                row = row_of(features, a)
                for part in range(2):
                    made[tile, a, part] = row[part * HALF : (part + 1) * HALF]
            copy = pltpu.make_async_copy(
                made.at[tile], gate_place(gate, tile), departures.at[tile]
            )
            copy.start()
        return carry

    lax.fori_loop(0, TILES // PAIR, body, 0)
    for t in range(TILES):
        pltpu.make_async_copy(made.at[t], gate_place(gate, t), departures.at[t]).wait()


def turn(weight):
    return weight[...].astype(F32).T


def pixel_kernel(
    picture, bias_pair,
    in_gain, in_weight, grid_gain, grid_wide, grid_gate_gain, grid_mixing, grid_narrow,
    block_gain, block_wide, out_weight,
    passed, kept, keys, base, final_weight, mixing_out,
    held, arrivals,
):
    fetch_tiles(picture, held, arrivals)

    place = lax.broadcasted_iota(jnp.int32, (CELLS, CELLS), 0)
    cell = lax.broadcasted_iota(jnp.int32, (CELLS, CELLS), 1)
    wanted = ((place // 32) * 2 + place % 2) * SIDE + (place // 2) % SIDE
    order = jnp.where(cell == wanted, 1.0, 0.0).astype(BF16)
    turned = mm_nt(order, grid_mixing[...]).astype(BF16)
    mixing_out[...] = mm_nt(turned, order).astype(BF16)

    out_turned = turn(out_weight)
    grid_both = mm_nt(out_turned[:, :C].astype(BF16), grid_narrow[...])
    final_weight[...] = fourfold(grid_both * grid_gate_gain[...])
    grid_plain = fourfold(grid_both)
    out_grid, out_block = fourfold(out_turned[:, :C]), fourfold(out_turned[:, C:])
    first = turn(in_weight)
    first_grid, first_block = fourfold(first[:C]), fourfold(first[C:])
    grid_pass_weight = fourfold(turn(grid_wide)[:C])
    block_both = turn(block_wide)
    block_pass_weight, block_gate_weight = fourfold(block_both[:C]), fourfold(block_both[C:])
    in_rows, grid_rows = on_rows(in_gain[...]), on_rows(grid_gain[...])
    block_rows = on_rows(block_gain[...])

    def body(step, carry):
        tiles = [step * PAIR + k for k in range(PAIR)]
        for tile in tiles:
            wait_tile(picture, held, arrivals, tile)
        values = [pixels(held[tile]) for tile in tiles]
        normed = [normalize(v, in_rows) for v in values]
        grid_hidden = [gelu(mm(first_grid, v)) for v in normed]
        block_hidden = [gelu(mm(first_block, v)) for v in normed]
        normed = [normalize(v, block_rows) for v in block_hidden]
        features = [gelu(mm(block_gate_weight, v)) for v in normed]
        for tile, v in zip(tiles, normed):
            kept[tile] = gelu(mm(block_pass_weight, v))
        features = [normalize(v) for v in features]
        for tile, v in zip(tiles, features):
            for g in range(GROUPS):
                keys[tile, :, g * WIDE : (g + 1) * WIDE] = v[g * C : (g + 1) * C]
        normed = [normalize(v, grid_rows) for v in grid_hidden]
        grid_pass = [gelu(mm(grid_pass_weight, v)) for v in normed]
        for k, tile in enumerate(tiles):
            passed[tile] = grid_pass[k]
            own = bias_pair[0, tile // QUARTERS] + 1.0
            part = mm(out_grid, grid_hidden[k]) + mm(out_block, block_hidden[k])
            part = part + mm(grid_plain, (grid_pass[k].astype(F32) * own).astype(BF16))
            base[tile] = values[k].astype(F32) + part
        return carry

    lax.fori_loop(0, TILES // PAIR, body, 0)


def block_kernel(
    token, kept, keys, total, block_mixing, block_bias, block_gate_gain, block_narrow, out_weight,
    base,
    spread, mixed,
):
    source = lax.broadcasted_iota(jnp.int32, (CELLS, STRIP), 0)
    target = lax.broadcasted_iota(jnp.int32, (CELLS, STRIP), 1)
    chosen = (target // LANES) * SIDE + target % SIDE
    pick = jnp.where(source == chosen, 1.0, 0.0).astype(BF16)
    expanded = mm(block_mixing[...], pick).astype(BF16)
    same = lax.broadcasted_iota(jnp.int32, (LANES, STRIP), 0) // SIDE == (
        lax.broadcasted_iota(jnp.int32, (LANES, STRIP), 1) % LANES
    ) // SIDE
    mask = jnp.where(same, 1.0, 0.0).astype(BF16)
    for p in range(SIDE):
        rows = expanded[p * SIDE : (p + 1) * SIDE]
        rows = jnp.concatenate([rows] * (LANES // SIDE), axis=0)
        spread[p * LANES : (p + 1) * LANES, :] = rows * mask
    bias = block_bias[...]
    coarse = bias.astype(BF16)
    fine = (bias - coarse.astype(F32)).astype(BF16)
    offset = mm(coarse, pick) + mm(fine, pick) + 1.0
    offset = jnp.concatenate(
        [jnp.broadcast_to(offset[:, g * WIDE : (g + 1) * WIDE], (C, WIDE)) for g in range(GROUPS)],
        axis=0,
    )
    block_both = mm_nt(turn(out_weight)[:, C:].astype(BF16), block_narrow[...])
    block_gained = fourfold(block_both * block_gate_gain[...])
    block_plain = fourfold(block_both)

    flat = keys[...].reshape(TILES * C, STRIP)

    def mix(step, carry):
        columns = pl.ds(pl.multiple_of(step * CELLS, CELLS), CELLS)
        mixed[:, columns] = mm(flat, spread[:, columns]).astype(BF16)
        return carry

    lax.fori_loop(0, STRIP // CELLS, mix, 0)

    def after(tile, carry):
        rows = pl.ds(pl.multiple_of(tile * C, C), C)
        blended = jnp.concatenate(
            [mixed[rows, g * WIDE : (g + 1) * WIDE] for g in range(GROUPS)], axis=0
        )
        through = kept[tile]
        part = mm(block_gained, through * blended)
        part = part + mm(block_plain, (through.astype(F32) * offset).astype(BF16))
        base[tile] = total[tile] + part
        return carry

    lax.fori_loop(0, TILES, after, 0, unroll=2)


def sent_place(sent, cell, step):
    return sent.at[:, cell, pl.ds(step * SIDE, SIDE), :]


def mix_kernel(arrived, mixing, sent, token, made, departures):
    weight = mixing[...]
    token[...] = jnp.zeros_like(token)
    copies = []
    for step in range(HALF // SIDE):
        cells = arrived[:, :, pl.ds(step * SIDE, SIDE), :].reshape(CELLS, SIDE, LANES)
        cells = pltpu.einshape("kcl->ckl", cells)
        results = []
        for c in range(0, SIDE, 2):
            result = mm(weight, jnp.concatenate([cells[c], cells[c + 1]], axis=1)).astype(BF16)
            results += [result[:, :LANES], result[:, LANES:]]
        results = pltpu.einshape("ckl->kcl", jnp.stack(results))
        made[step] = results.reshape(PEERS, 2, SIDE, LANES)
        for cell in range(2):
            copy = pltpu.make_async_copy(
                made.at[step, :, cell], sent_place(sent, cell, step), departures.at[step, cell]
            )
            copy.start()
            copies.append(copy)
    for copy in copies:
        copy.wait()


def final_kernel(
    returned, passed_in, base_in, weight,
    refined,
    passed, base, made, arrivals, departures,
):
    def coming(tile):
        return [
            pltpu.make_async_copy(passed_in.at[tile], passed.at[tile], arrivals.at[tile, 0]),
            pltpu.make_async_copy(base_in.at[tile], base.at[tile], arrivals.at[tile, 1]),
        ]

    for t in range(TILES):
        for copy in coming(t):
            copy.start()
    final = weight[...]

    def blended(tile):
        cell = tile // QUARTERS
        quarter = tile % QUARTERS
        rows = pl.ds(pl.multiple_of(cell * HALF, HALF), HALF)
        return stack(
            [
                jnp.concatenate(
                    [returned[a, quarter, 0, rows, :], returned[a, quarter, 1, rows, :]], axis=0
                )
                for a in range(SIDE)
            ]
        )

    def body(step, carry):
        tiles = [step * PAIR + k for k in range(PAIR)]
        for tile in tiles:
            for copy in coming(tile):
                copy.wait()
        values = [passed[tile] * blended(tile) for tile in tiles]
        values = [mm(final, v) for v in values]
        values = [(base[tile] + v).astype(BF16) for tile, v in zip(tiles, values)]
        for tile, v in zip(tiles, values):
            rows = jnp.stack([row_of(v, a) for a in range(SIDE)])
            made[tile] = pltpu.einshape("rcl->crl", rows)
        for tile in tiles:
            pltpu.make_async_copy(
                made.at[tile], refined.at[place_of(tile)], departures.at[tile]
            ).start()
        return carry

    lax.fori_loop(0, TILES // PAIR, body, 0)
    for t in range(TILES):
        pltpu.make_async_copy(made.at[t], refined.at[place_of(t)], departures.at[t]).wait()


VMEM, SMEM, HBM = pltpu.VMEM, pltpu.SMEM, pltpu.HBM


def kernel_call(kernel, name, places, outputs, scratch, limit, flops, *operands):
    operands = [
        pltpu.with_memory_space_constraint(value, place) if place in (HBM, VMEM) else value
        for value, place in zip(operands, places)
    ]
    return pl.pallas_call(
        kernel,
        in_specs=[pl.BlockSpec(memory_space=place or VMEM) for place in places],
        out_specs=[pl.BlockSpec(memory_space=place) for _, _, place in outputs],
        out_shape=[place(shape, kind) for shape, kind, place in outputs],
        scratch_shapes=scratch,
        name=name,
        cost_estimate=pl.CostEstimate(flops=flops, bytes_accessed=1 << 22, transcendentals=0),
        compiler_params=pltpu.CompilerParams(vmem_limit_bytes=limit << 20),
    )(*operands)


def exchange(values):
    pieces = values.reshape(PEERS, C, LANES)
    pieces = lax.all_to_all(pieces, ("row", "col"), split_axis=0, concat_axis=0, tiled=True)
    return pieces


GATE_SHAPE = (SIDE, QUARTERS, 2, C, LANES)
CELL_SHAPE = (PEERS, 2, HALF, LANES)
STACKED = (TILES, DEEP, WIDE)
KEYS = (TILES, C, STRIP)
BLOCKS = (TILES, C, SIDE, LANES)
DMA = pltpu.SemaphoreType.DMA


def gate_call(picture, in_gain, in_weight, wide_gain, wide_weight):
    return kernel_call(
        gate_kernel, "gate", [HBM] * 5, [(GATE_SHAPE, BF16, HBM)],
        [
            VMEM(BLOCKS, BF16),
            VMEM((TILES, SIDE, 2, HALF, LANES), BF16),
            VMEM((2, 1, C), F32),
            VMEM((2, C, 2 * C), BF16),
            DMA((TILES,)), DMA((TILES,)), DMA((4,)),
        ],
        24, 1 << 30, picture, in_gain, in_weight, wide_gain, wide_weight,
    )[0]


def pixel_call(*operands):
    return kernel_call(
        pixel_kernel, "pixel", [HBM, SMEM] + [None] * 10,
        [
            (STACKED, BF16, VMEM), (STACKED, BF16, VMEM), (KEYS, BF16, VMEM), (STACKED, F32, VMEM),
            ((DEEP, DEEP), BF16, VMEM), ((CELLS, CELLS), BF16, VMEM),
        ],
        [VMEM(BLOCKS, BF16), DMA((TILES,))],
        24, 20 << 30, *operands,
    )


def block_call(*operands):
    return kernel_call(
        block_kernel, "block", [VMEM] * 4 + [None] * 5,
        [(STACKED, F32, VMEM)],
        [VMEM((STRIP, STRIP), BF16), VMEM((TILES * C, STRIP), BF16)],
        24, 20 << 30, *operands,
    )[0]


def mix_call(arrived, mixing):
    return kernel_call(
        mix_kernel, "mix", [VMEM, VMEM],
        [(CELL_SHAPE, BF16, HBM), ((8, LANES), F32, VMEM)],
        [VMEM((HALF // SIDE, PEERS, 2, SIDE, LANES), BF16), DMA((HALF // SIDE, 2))],
        16, 1 << 30, arrived, mixing,
    )


def final_call(returned, passed, base, weight, shape):
    return kernel_call(
        final_kernel, "final", [VMEM, HBM, HBM, VMEM], [(shape, BF16, HBM)],
        [
            VMEM(STACKED, BF16), VMEM(STACKED, F32), VMEM(BLOCKS, BF16),
            DMA((TILES, 2)), DMA((TILES,)),
        ],
        24, 1 << 30, returned, passed, base, weight,
    )[0]


def on_device(
    picture,
    input_gain,
    input_weight,
    grid_branch_scale,
    grid_widen_weight,
    grid_gate_scale,
    grid_mixing,
    grid_bias,
    grid_narrow_weight,
    block_branch_scale,
    block_widen_weight,
    block_gate_scale,
    block_mixing,
    block_bias,
    block_narrow_weight,
    output_weight,
):
    row = lambda gain: gain.reshape(1, -1)
    gate = gate_call(
        picture, row(input_gain), input_weight, row(grid_branch_scale), grid_widen_weight
    )
    arrived = exchange(gate).reshape(CELL_SHAPE)
    position = lax.axis_index("row") * 2 * SIDE + lax.axis_index("col")
    own_bias = jnp.stack(
        [
            lax.dynamic_index_in_dim(grid_bias, position, keepdims=False),
            lax.dynamic_index_in_dim(grid_bias, position + SIDE, keepdims=False),
        ]
    ).reshape(1, 2)
    passed, kept, keys, base, final_weight, mixing = pixel_call(
        picture, own_bias,
        row(input_gain), input_weight,
        row(grid_branch_scale), grid_widen_weight, row(grid_gate_scale), grid_mixing,
        grid_narrow_weight,
        row(block_branch_scale), block_widen_weight, output_weight,
    )
    sent, token = mix_call(arrived, mixing)
    returned = exchange(sent).reshape(GATE_SHAPE)
    base = block_call(
        token, kept, keys, base, block_mixing, row(block_bias), row(block_gate_scale),
        block_narrow_weight, output_weight,
    )
    return final_call(returned, passed, base, final_weight, picture.shape)


def solution(mesh):
    return jax.shard_map(
        on_device,
        mesh=mesh,
        in_specs=(P(None, "row", "col"),) + (P(),) * 15,
        out_specs=P(None, "row", "col"),
        check_vma=False,
    )
```

```python
import jax
import jax.numpy as jnp
from jax import lax
from jax.experimental import pallas as pl
from jax.experimental.pallas import tpu as pltpu
from jax.sharding import PartitionSpec as P

F32 = jnp.float32
BF16 = jnp.bfloat16
C = 64
SIDE = 16
CELLS = 256
LANES = 128
COLS = 512
QUARTERS = COLS // LANES
TILES = 2 * QUARTERS
STRIP = SIDE * LANES
PEERS = 128
PAIR = 2
HALF = C // 2
GROUPS = 4
DEEP = GROUPS * C
WIDE = STRIP // GROUPS
EPSILON = 1e-06
GELU_A = 0.7978845608
GELU_B = 0.7978845608 * 0.044715
SCALE = GELU_B ** (1 / 3)
BEND = GELU_A / SCALE
HEAD = 2
MIX_PARTS = 2


def mm(a, b):
    return jnp.dot(a, b, preferred_element_type=F32)


def mm_nt(a, b):
    return lax.dot_general(a, b, (((1,), (1,)), ((), ())), preferred_element_type=F32)


def short(value):
    return jnp.array(value, BF16)


def normalize(values, gain=None):
    n = values.shape[1]
    values = values.astype(F32).reshape(GROUPS, C, n)
    centered = values - jnp.sum(values, axis=1, keepdims=True) * (1.0 / C)
    spread = jnp.sum(centered * centered, axis=1, keepdims=True) * (1.0 / C)
    centered = centered * lax.rsqrt(spread + EPSILON)
    if gain is not None:
        centered = centered * gain[None]
    return centered.astype(BF16).reshape(DEEP, n)


def gelu(values):
    bend = jnp.tanh(values * (GELU_B * (values * values) + GELU_A))
    half = 0.5 * values
    return (half * bend + half).astype(BF16)


def gelu_scaled(values):
    u = values.astype(BF16)
    return u * jnp.tanh(u * (u * u + short(BEND))) + u


def normalize_picture(values):
    n = values.shape[1]
    values = values.astype(F32).reshape(GROUPS, C, n)
    centered = values - jnp.sum(values, axis=1, keepdims=True) * (1.0 / C)
    spread = jnp.sum(centered * centered, axis=1, keepdims=True)
    return (centered * lax.rsqrt(spread + C * EPSILON)).astype(BF16).reshape(DEEP, n)


def normalize_scaled(values):
    n = values.shape[1]
    values = values.astype(F32).reshape(GROUPS, C, n)
    centered = (values - jnp.sum(values, axis=1, keepdims=True) * (1.0 / C)).astype(BF16)
    centered = centered.reshape(GROUPS, C // SIDE, SIDE, n)
    spread = centered * centered
    spread = ((spread[:, 0] + spread[:, 1]) + (spread[:, 2] + spread[:, 3])).astype(F32)
    spread = jnp.sum(spread, axis=1, keepdims=True)
    factor = lax.rsqrt(spread + C * EPSILON * (4.0 * SCALE * SCALE))
    factor = jnp.broadcast_to(factor, (GROUPS, SIDE, n)).astype(BF16)
    return (centered * factor[:, None]).reshape(DEEP, n)


def fourfold(weight):
    wide = jnp.concatenate([weight.astype(BF16)] * GROUPS, axis=1)
    wide = jnp.concatenate([wide] * GROUPS, axis=0)
    rows = lax.broadcasted_iota(jnp.int32, (DEEP, DEEP), 0) // C
    columns = lax.broadcasted_iota(jnp.int32, (DEEP, DEEP), 1) // C
    return wide * jnp.where(rows == columns, 1.0, 0.0).astype(BF16)


def on_rows(gain):
    block = jnp.broadcast_to(gain, (LANES, C)).T
    return jnp.concatenate([block] * (WIDE // LANES), axis=1)


def place_of(tile):
    rows = pl.ds(pl.multiple_of(tile // QUARTERS * SIDE, SIDE), SIDE)
    lanes = pl.ds(pl.multiple_of(tile % QUARTERS * LANES, LANES), LANES)
    return slice(None), rows, lanes


def stack(rows):
    step = SIDE // GROUPS
    groups = [
        jnp.concatenate([rows[g * step + j] for j in range(step)], axis=1) for g in range(GROUPS)
    ]
    return jnp.concatenate(groups, axis=0)


def row_of(values, r):
    step = SIDE // GROUPS
    g, j = r // step, r % step
    return values[g * C : (g + 1) * C, j * LANES : (j + 1) * LANES]


def pixels(block):
    return stack(pltpu.einshape("crl->rcl", block))


def fetch_tiles(picture, held, arrivals):
    copies = [
        pltpu.make_async_copy(picture.at[place_of(t)], held.at[t], arrivals.at[t])
        for t in range(TILES)
    ]
    for copy in copies:
        copy.start()


def wait_tile(picture, held, arrivals, tile):
    pltpu.make_async_copy(picture.at[place_of(tile)], held.at[tile], arrivals.at[tile]).wait()


def gate_place(gate, tile):
    cell, quarter = tile // QUARTERS, tile % QUARTERS
    return gate.at[:, quarter, :, pl.ds(pl.multiple_of(cell * HALF, HALF), HALF), :]


def gate_kernel(
    picture, in_gain, in_weight, wide_gain, wide_weight,
    gate,
    held, made, gains, weights, arrivals, departures, small,
):
    parts = [
        pltpu.make_async_copy(in_weight, weights.at[0], small.at[0]),
        pltpu.make_async_copy(wide_weight, weights.at[1], small.at[1]),
        pltpu.make_async_copy(in_gain, gains.at[0], small.at[2]),
        pltpu.make_async_copy(wide_gain, gains.at[1], small.at[3]),
    ]
    for copy in parts:
        copy.start()
    fetch_tiles(picture, held, arrivals)
    for copy in parts:
        copy.wait()
    first = fourfold(weights[0].astype(F32).T[:C] * (gains[0] * (8.0 * SCALE)))
    second = fourfold(weights[1].astype(F32).T[C:] * (gains[1] * (8.0 * SCALE)))

    def body(step, carry):
        tiles = [step * PAIR + k for k in range(PAIR)]
        for tile in tiles:
            wait_tile(picture, held, arrivals, tile)
        values = [normalize_picture(pixels(held[tile])) for tile in tiles]
        values = [gelu_scaled(mm(first, v)) for v in values]
        values = [normalize_scaled(v) for v in values]
        values = [gelu_scaled(mm(second, v)) for v in values]
        values = [normalize_scaled(v) for v in values]
        for tile, features in zip(tiles, values):
            for a in range(SIDE):
                row = row_of(features, a)
                for part in range(2):
                    made[tile, a, part] = row[part * HALF : (part + 1) * HALF]
            copy = pltpu.make_async_copy(
                made.at[tile], gate_place(gate, tile), departures.at[tile]
            )
            copy.start()
        return carry

    lax.fori_loop(0, TILES // PAIR, body, 0)
    for t in range(TILES):
        pltpu.make_async_copy(made.at[t], gate_place(gate, t), departures.at[t]).wait()


def turn(weight):
    return weight[...].astype(F32).T


def pixel_kernel(
    picture, grid_bias,
    in_gain, in_weight, grid_gain, grid_wide, grid_gate_gain, grid_mixing, grid_narrow,
    block_gain, block_wide, out_weight,
    passed_out, kept_out, keys_out, total_out, final_weight, mixing_out,
    held, passed, kept, keys, total, arrivals, departures,
):
    fetch_tiles(picture, held, arrivals)

    place = lax.broadcasted_iota(jnp.int32, (CELLS, CELLS), 0)
    cell = lax.broadcasted_iota(jnp.int32, (CELLS, CELLS), 1)
    wanted = ((place // 32) * 2 + place % 2) * SIDE + (place // 2) % SIDE
    order = jnp.where(cell == wanted, 1.0, 0.0).astype(BF16)
    turned = mm_nt(order, grid_mixing[...]).astype(BF16)
    mixing_out[...] = mm_nt(turned, order).astype(BF16)

    out_turned = turn(out_weight)
    grid_both = mm_nt(out_turned[:, :C].astype(BF16), grid_narrow[...])
    final_weight[...] = fourfold(grid_both * (grid_gate_gain[...] * 8.0))
    grid_plain = fourfold(grid_both)
    out_grid, out_block = fourfold(out_turned[:, :C]), fourfold(out_turned[:, C:])
    first = turn(in_weight)
    first_grid, first_block = fourfold(first[:C]), fourfold(first[C:])
    grid_pass_weight = fourfold(turn(grid_wide)[:C])
    block_both = turn(block_wide)
    block_pass_weight, block_gate_weight = fourfold(block_both[:C]), fourfold(block_both[C:])
    in_rows, grid_rows = on_rows(in_gain[...]), on_rows(grid_gain[...])
    block_rows = on_rows(block_gain[...])
    own_cell = lax.axis_index("row") * 2 * SIDE + lax.axis_index("col")
    lane = lax.broadcasted_iota(jnp.int32, (1, CELLS), 1)

    def leaving(tile):
        pairs = [(passed, passed_out), (kept, kept_out), (keys, keys_out), (total, total_out)]
        return [
            pltpu.make_async_copy(made.at[tile], out.at[tile], departures.at[tile, k])
            for k, (made, out) in enumerate(pairs)
        ]

    def body(step, carry):
        tiles = [step * PAIR + k for k in range(PAIR)]
        for tile in tiles:
            wait_tile(picture, held, arrivals, tile)
        values = [pixels(held[tile]) for tile in tiles]
        normed = [normalize(v, in_rows) for v in values]
        grid_hidden = [gelu(mm(first_grid, v)) for v in normed]
        block_hidden = [gelu(mm(first_block, v)) for v in normed]
        normed = [normalize(v, block_rows) for v in block_hidden]
        features = [gelu(mm(block_gate_weight, v)) for v in normed]
        for tile, v in zip(tiles, normed):
            kept[tile] = gelu(mm(block_pass_weight, v))
        features = [normalize(v) for v in features]
        for tile, v in zip(tiles, features):
            for g in range(GROUPS):
                keys[tile, :, g * WIDE : (g + 1) * WIDE] = v[g * C : (g + 1) * C]
        normed = [normalize(v, grid_rows) for v in grid_hidden]
        grid_pass = [gelu(mm(grid_pass_weight, v)) for v in normed]
        for k, tile in enumerate(tiles):
            passed[tile] = grid_pass[k]
            cell = own_cell + tile // QUARTERS * SIDE
            own = jnp.sum(jnp.where(lane == cell, grid_bias[...], 0.0), axis=1, keepdims=True) + 1.0
            part = mm(out_grid, grid_hidden[k]) + mm(out_block, block_hidden[k])
            part = part + mm(grid_plain, (grid_pass[k].astype(F32) * own).astype(BF16))
            total[tile] = values[k].astype(F32) + part
        for tile in tiles:
            for copy in leaving(tile):
                copy.start()
        return carry

    lax.fori_loop(0, TILES // PAIR, body, 0)
    for t in range(TILES):
        for copy in leaving(t):
            copy.wait()


def block_kernel(
    token, passed_in, kept_in, keys_in, total_in,
    block_mixing, block_bias, block_gate_gain, block_narrow, out_weight,
    passed_head, base_head, base_out,
    spread, mixed, kept, keys, total, base, arrivals, departures,
):
    def coming(tile):
        pairs = [(keys_in, keys), (kept_in, kept), (total_in, total)]
        return [
            pltpu.make_async_copy(there.at[tile], here.at[tile], arrivals.at[tile, k])
            for k, (there, here) in enumerate(pairs)
        ]

    def head(tile):
        return pltpu.make_async_copy(
            passed_in.at[tile], passed_head.at[tile], arrivals.at[tile, 3]
        )

    def leaving(tile):
        return pltpu.make_async_copy(base.at[tile], base_out.at[tile], departures.at[tile])

    for t in range(TILES):
        for copy in coming(t):
            copy.start()
    for t in range(HEAD):
        head(t).start()

    source = lax.broadcasted_iota(jnp.int32, (CELLS, STRIP), 0)
    target = lax.broadcasted_iota(jnp.int32, (CELLS, STRIP), 1)
    chosen = (target // LANES) * SIDE + target % SIDE
    pick = jnp.where(source == chosen, 1.0, 0.0).astype(BF16)
    expanded = mm(block_mixing[...], pick).astype(BF16)
    same = lax.broadcasted_iota(jnp.int32, (LANES, STRIP), 0) // SIDE == (
        lax.broadcasted_iota(jnp.int32, (LANES, STRIP), 1) % LANES
    ) // SIDE
    mask = jnp.where(same, 1.0, 0.0).astype(BF16)
    for p in range(SIDE):
        rows = expanded[p * SIDE : (p + 1) * SIDE]
        rows = jnp.concatenate([rows] * (LANES // SIDE), axis=0)
        spread[p * LANES : (p + 1) * LANES, :] = rows * mask
    bias = block_bias[...]
    coarse = bias.astype(BF16)
    fine = (bias - coarse.astype(F32)).astype(BF16)
    offset = mm(coarse, pick) + mm(fine, pick) + 1.0
    offset = jnp.concatenate(
        [jnp.broadcast_to(offset[:, g * WIDE : (g + 1) * WIDE], (C, WIDE)) for g in range(GROUPS)],
        axis=0,
    )
    block_both = mm_nt(turn(out_weight)[:, C:].astype(BF16), block_narrow[...])
    block_gained = fourfold(block_both * block_gate_gain[...])
    block_plain = fourfold(block_both)

    for t in range(TILES):
        for copy in coming(t):
            copy.wait()
    for t in range(HEAD):
        head(t).wait()
    flat = keys[...].reshape(TILES * C, STRIP)

    def mix(step, carry):
        columns = pl.ds(pl.multiple_of(step * CELLS, CELLS), CELLS)
        mixed[:, columns] = mm(flat, spread[:, columns]).astype(BF16)
        return carry

    lax.fori_loop(0, STRIP // CELLS, mix, 0)

    def after(tile, carry):
        rows = pl.ds(pl.multiple_of(tile * C, C), C)
        blended = jnp.concatenate(
            [mixed[rows, g * WIDE : (g + 1) * WIDE] for g in range(GROUPS)], axis=0
        )
        through = kept[tile]
        part = mm(block_gained, through * blended)
        part = part + mm(block_plain, (through.astype(F32) * offset).astype(BF16))
        base[tile] = (total[tile] + part).astype(BF16)
        leaving(tile).start()
        return carry

    lax.fori_loop(0, TILES, after, 0)
    for t in range(TILES):
        leaving(t).wait()
    for t in range(HEAD):
        base_head[t] = base[t]


def sent_place(sent, cell, step, part):
    count = PEERS // MIX_PARTS
    return sent.at[pl.ds(part * count, count), cell, pl.ds(step * SIDE, SIDE), :]


def mix_kernel(arrived, mixing, sent, token, made, departures):
    weight = mixing[...]
    token[...] = jnp.zeros_like(token)
    count = PEERS // MIX_PARTS
    copies = []
    for step in range(HALF // SIDE):
        cells = arrived[:, :, pl.ds(step * SIDE, SIDE), :].reshape(CELLS, SIDE, LANES)
        cells = pltpu.einshape("kcl->ckl", cells)
        results = []
        for c in range(0, SIDE, 2):
            result = mm(weight, jnp.concatenate([cells[c], cells[c + 1]], axis=1)).astype(BF16)
            results += [result[:, :LANES], result[:, LANES:]]
        for part in range(MIX_PARTS):
            rows = slice(part * 2 * count, (part + 1) * 2 * count)
            mixed = pltpu.einshape("ckl->kcl", jnp.stack([r[rows] for r in results]))
            made[step, part] = mixed.reshape(count, 2, SIDE, LANES)
            for cell in range(2):
                copy = pltpu.make_async_copy(
                    made.at[step, part, :, cell],
                    sent_place(sent, cell, step, part),
                    departures.at[step, part, cell],
                )
                copy.start()
                copies.append(copy)
    for copy in copies:
        copy.wait()


def final_kernel(
    returned, passed_head, base_head, passed_in, base_in, weight,
    refined,
    passed, base, made, arrivals, departures,
):
    def coming(tile):
        return [
            pltpu.make_async_copy(passed_in.at[tile], passed.at[tile], arrivals.at[tile, 0]),
            pltpu.make_async_copy(base_in.at[tile], base.at[tile], arrivals.at[tile, 1]),
        ]

    for t in range(HEAD, TILES):
        for copy in coming(t):
            copy.start()
    final = weight[...]

    def blended(tile):
        cell = tile // QUARTERS
        quarter = tile % QUARTERS
        rows = pl.ds(pl.multiple_of(cell * HALF, HALF), HALF)
        return stack(
            [
                jnp.concatenate(
                    [returned[a, quarter, 0, rows, :], returned[a, quarter, 1, rows, :]], axis=0
                )
                for a in range(SIDE)
            ]
        )

    def finish(tiles, passed, base):
        values = [passed[tile] * blended(tile) for tile in tiles]
        values = [mm(final, v) for v in values]
        values = [(base[tile].astype(F32) + v).astype(BF16) for tile, v in zip(tiles, values)]
        for tile, v in zip(tiles, values):
            rows = jnp.stack([row_of(v, a) for a in range(SIDE)])
            made[tile] = pltpu.einshape("rcl->crl", rows)
        for tile in tiles:
            pltpu.make_async_copy(
                made.at[tile], refined.at[place_of(tile)], departures.at[tile]
            ).start()

    finish([jnp.int32(t) for t in range(HEAD)], passed_head, base_head)

    def body(step, carry):
        tiles = [HEAD + step * PAIR + k for k in range(PAIR)]
        for tile in tiles:
            for copy in coming(tile):
                copy.wait()
        finish(tiles, passed, base)
        return carry

    lax.fori_loop(0, (TILES - HEAD) // PAIR, body, 0)
    for t in range(TILES):
        pltpu.make_async_copy(made.at[t], refined.at[place_of(t)], departures.at[t]).wait()


VMEM, SMEM, HBM = pltpu.VMEM, pltpu.SMEM, pltpu.HBM


def kernel_call(kernel, name, places, outputs, scratch, limit, flops, *operands):
    operands = [
        pltpu.with_memory_space_constraint(value, place) if place in (HBM, VMEM) else value
        for value, place in zip(operands, places)
    ]
    return pl.pallas_call(
        kernel,
        in_specs=[pl.BlockSpec(memory_space=place or VMEM) for place in places],
        out_specs=[pl.BlockSpec(memory_space=place) for _, _, place in outputs],
        out_shape=[place(shape, kind) for shape, kind, place in outputs],
        scratch_shapes=scratch,
        name=name,
        cost_estimate=pl.CostEstimate(flops=flops, bytes_accessed=1 << 22, transcendentals=0),
        compiler_params=pltpu.CompilerParams(vmem_limit_bytes=limit << 20),
    )(*operands)


def exchange(values):
    pieces = values.reshape(PEERS, C, LANES)
    pieces = lax.all_to_all(pieces, ("row", "col"), split_axis=0, concat_axis=0, tiled=True)
    return pieces


GATE_SHAPE = (SIDE, QUARTERS, 2, C, LANES)
CELL_SHAPE = (PEERS, 2, HALF, LANES)
STACKED = (TILES, DEEP, WIDE)
KEYS = (TILES, C, STRIP)
BLOCKS = (TILES, C, SIDE, LANES)
DMA = pltpu.SemaphoreType.DMA


def gate_call(picture, in_gain, in_weight, wide_gain, wide_weight):
    return kernel_call(
        gate_kernel, "gate", [HBM] * 5, [(GATE_SHAPE, BF16, HBM)],
        [
            VMEM(BLOCKS, BF16),
            VMEM((TILES, SIDE, 2, HALF, LANES), BF16),
            VMEM((2, 1, C), F32),
            VMEM((2, C, 2 * C), BF16),
            DMA((TILES,)), DMA((TILES,)), DMA((4,)),
        ],
        24, 1 << 30, picture, in_gain, in_weight, wide_gain, wide_weight,
    )[0]


HEADS = (HEAD, DEEP, WIDE)


def pixel_call(*operands):
    return kernel_call(
        pixel_kernel, "pixel", [HBM] + [None] * 11,
        [
            (STACKED, BF16, HBM), (STACKED, BF16, HBM), (KEYS, BF16, HBM), (STACKED, F32, HBM),
            ((DEEP, DEEP), BF16, VMEM), ((CELLS, CELLS), BF16, VMEM),
        ],
        [
            VMEM(BLOCKS, BF16), VMEM(STACKED, BF16), VMEM(STACKED, BF16), VMEM(KEYS, BF16),
            VMEM(STACKED, F32), DMA((TILES,)), DMA((TILES, 4)),
        ],
        32, 20 << 30, *operands,
    )


def block_call(*operands):
    return kernel_call(
        block_kernel, "block", [VMEM] + [HBM] * 4 + [None] * 5,
        [(HEADS, BF16, VMEM), (HEADS, BF16, VMEM), (STACKED, BF16, HBM)],
        [
            VMEM((STRIP, STRIP), BF16), VMEM((TILES * C, STRIP), BF16), VMEM(STACKED, BF16),
            VMEM(KEYS, BF16), VMEM(STACKED, F32), VMEM(STACKED, BF16),
            DMA((TILES, 4)), DMA((TILES,)),
        ],
        40, 20 << 30, *operands,
    )


def mix_call(arrived, mixing):
    return kernel_call(
        mix_kernel, "mix", [VMEM, VMEM],
        [(CELL_SHAPE, BF16, HBM), ((8, LANES), F32, VMEM)],
        [
            VMEM((HALF // SIDE, MIX_PARTS, PEERS // MIX_PARTS, 2, SIDE, LANES), BF16),
            DMA((HALF // SIDE, MIX_PARTS, 2)),
        ],
        16, 1 << 30, arrived, mixing,
    )


def final_call(returned, passed_head, base_head, passed, base, weight, shape):
    return kernel_call(
        final_kernel, "final", [VMEM, VMEM, VMEM, HBM, HBM, VMEM], [(shape, BF16, HBM)],
        [
            VMEM(STACKED, BF16), VMEM(STACKED, BF16), VMEM(BLOCKS, BF16),
            DMA((TILES, 2)), DMA((TILES,)),
        ],
        24, 1 << 30, returned, passed_head, base_head, passed, base, weight,
    )[0]


def on_device(
    picture,
    input_gain,
    input_weight,
    grid_branch_scale,
    grid_widen_weight,
    grid_gate_scale,
    grid_mixing,
    grid_bias,
    grid_narrow_weight,
    block_branch_scale,
    block_widen_weight,
    block_gate_scale,
    block_mixing,
    block_bias,
    block_narrow_weight,
    output_weight,
):
    row = lambda gain: gain.reshape(1, -1)
    gate = gate_call(
        picture, row(input_gain), input_weight, row(grid_branch_scale), grid_widen_weight
    )
    arrived = exchange(gate).reshape(CELL_SHAPE)
    passed, kept, keys, total, final_weight, mixing = pixel_call(
        picture, row(grid_bias),
        row(input_gain), input_weight,
        row(grid_branch_scale), grid_widen_weight, row(grid_gate_scale), grid_mixing,
        grid_narrow_weight,
        row(block_branch_scale), block_widen_weight, output_weight,
    )
    sent, token = mix_call(arrived, mixing)
    returned = exchange(sent).reshape(GATE_SHAPE)
    passed_head, base_head, base = block_call(
        token, passed, kept, keys, total, block_mixing, row(block_bias), row(block_gate_scale),
        block_narrow_weight, output_weight,
    )
    return final_call(
        returned, passed_head, base_head, passed, base, final_weight, picture.shape
    )


def solution(mesh):
    return jax.shard_map(
        on_device,
        mesh=mesh,
        in_specs=(P(None, "row", "col"),) + (P(),) * 15,
        out_specs=P(None, "row", "col"),
        check_vma=False,
    )
```

```python
import jax
import jax.numpy as jnp
from jax import lax
from jax.experimental import pallas as pl
from jax.experimental.pallas import tpu as pltpu
from jax.sharding import PartitionSpec as P

F32 = jnp.float32
BF16 = jnp.bfloat16
C = 64
SIDE = 16
CELLS = 256
LANES = 128
COLS = 512
QUARTERS = COLS // LANES
TILES = 2 * QUARTERS
STRIP = SIDE * LANES
PEERS = 128
PAIR = 2
HALF = C // 2
GROUPS = 4
DEEP = GROUPS * C
WIDE = STRIP // GROUPS
EPSILON = 1e-06
GELU_A = 0.7978845608
GELU_B = 0.7978845608 * 0.044715
SCALE = GELU_B ** (1 / 3)
BEND = GELU_A / SCALE
HEAD = 2
MIX_PARTS = 2
HALVES = 2
HALF_STEP = SIDE // GROUPS // HALVES


def mm(a, b):
    return jnp.dot(a, b, preferred_element_type=F32)


def mm_nt(a, b):
    return lax.dot_general(a, b, (((1,), (1,)), ((), ())), preferred_element_type=F32)


def short(value):
    return jnp.array(value, BF16)


def normalize(values, gain=None):
    n = values.shape[1]
    values = values.astype(F32).reshape(GROUPS, C, n)
    centered = values - jnp.sum(values, axis=1, keepdims=True) * (1.0 / C)
    spread = jnp.sum(centered * centered, axis=1, keepdims=True) * (1.0 / C)
    centered = centered * lax.rsqrt(spread + EPSILON)
    if gain is not None:
        centered = centered * gain[None]
    return centered.astype(BF16).reshape(DEEP, n)


def gelu(values):
    bend = jnp.tanh(values * (GELU_B * (values * values) + GELU_A))
    half = 0.5 * values
    return (half * bend + half).astype(BF16)


def gelu_scaled(values):
    u = values.astype(BF16)
    return u * jnp.tanh(u * (u * u + short(BEND))) + u


def channel_sums(values):
    quads = (values[:, 0] + values[:, 1]) + (values[:, 2] + values[:, 3])
    return jnp.sum(quads.astype(F32), axis=1, keepdims=True)


def normalize_short(values, epsilon):
    n = values.shape[1]
    values = values.reshape(GROUPS, C // SIDE, SIDE, n)
    mean = jnp.broadcast_to(channel_sums(values) * (1.0 / C), (GROUPS, SIDE, n))
    high = mean.astype(BF16)
    low = (mean - high.astype(F32)).astype(BF16)
    centered = (values - high[:, None]) - low[:, None]
    factor = lax.rsqrt(channel_sums(centered * centered) + C * epsilon)
    factor = jnp.broadcast_to(factor, (GROUPS, SIDE, n)).astype(BF16)
    return (centered * factor[:, None]).reshape(DEEP, n)


def centered_weight(weight, gain):
    weight = weight * (gain * (8.0 * SCALE))
    return fourfold(weight - jnp.sum(weight, axis=1, keepdims=True) * (1.0 / C))


def fourfold(weight):
    wide = jnp.concatenate([weight.astype(BF16)] * GROUPS, axis=1)
    wide = jnp.concatenate([wide] * GROUPS, axis=0)
    rows = lax.broadcasted_iota(jnp.int32, (DEEP, DEEP), 0) // C
    columns = lax.broadcasted_iota(jnp.int32, (DEEP, DEEP), 1) // C
    return wide * jnp.where(rows == columns, 1.0, 0.0).astype(BF16)


def on_rows(gain):
    block = jnp.broadcast_to(gain, (LANES, C)).T
    return jnp.concatenate([block] * (WIDE // LANES), axis=1)


def place_of(tile):
    rows = pl.ds(pl.multiple_of(tile // QUARTERS * SIDE, SIDE), SIDE)
    lanes = pl.ds(pl.multiple_of(tile % QUARTERS * LANES, LANES), LANES)
    return slice(None), rows, lanes


def stack(rows):
    step = SIDE // GROUPS
    groups = [
        jnp.concatenate([rows[g * step + j] for j in range(step)], axis=1) for g in range(GROUPS)
    ]
    return jnp.concatenate(groups, axis=0)


def half_rows(half):
    step = SIDE // GROUPS
    return [g * step + half * HALF_STEP + j for g in range(GROUPS) for j in range(HALF_STEP)]


def stack_half(rows, half):
    chosen = [rows[a] for a in half_rows(half)]
    groups = [
        jnp.concatenate(chosen[g * HALF_STEP : (g + 1) * HALF_STEP], axis=1)
        for g in range(GROUPS)
    ]
    return jnp.concatenate(groups, axis=0)


def row_of(values, r):
    step = SIDE // GROUPS
    g, j = r // step, r % step
    return values[g * C : (g + 1) * C, j * LANES : (j + 1) * LANES]


def pixels(block):
    return stack(pltpu.einshape("crl->rcl", block))


def fetch_tiles(picture, held, arrivals):
    copies = [
        pltpu.make_async_copy(picture.at[place_of(t)], held.at[t], arrivals.at[t])
        for t in range(TILES)
    ]
    for copy in copies:
        copy.start()


def wait_tile(picture, held, arrivals, tile):
    pltpu.make_async_copy(picture.at[place_of(tile)], held.at[tile], arrivals.at[tile]).wait()


def gate_place(gate, tile):
    cell, quarter = tile // QUARTERS, tile % QUARTERS
    return gate.at[:, quarter, :, pl.ds(pl.multiple_of(cell * HALF, HALF), HALF), :]


def gate_kernel(
    picture, in_gain, in_weight, wide_gain, wide_weight,
    gate,
    held, made, gains, weights, arrivals, departures, small,
):
    parts = [
        pltpu.make_async_copy(in_weight, weights.at[0], small.at[0]),
        pltpu.make_async_copy(wide_weight, weights.at[1], small.at[1]),
        pltpu.make_async_copy(in_gain, gains.at[0], small.at[2]),
        pltpu.make_async_copy(wide_gain, gains.at[1], small.at[3]),
    ]
    for copy in parts:
        copy.start()
    fetch_tiles(picture, held, arrivals)
    for copy in parts:
        copy.wait()
    first = centered_weight(weights[0].astype(F32).T[:C], gains[0])
    second = centered_weight(weights[1].astype(F32).T[C:], gains[1])

    def body(step, carry):
        tiles = [step * PAIR + k for k in range(PAIR)]
        for tile in tiles:
            wait_tile(picture, held, arrivals, tile)
        rows = {}

        def load(unit):
            tile, half = tiles[unit // HALVES], unit % HALVES
            if half == 0:
                rows[unit // HALVES] = pltpu.einshape("crl->rcl", held[tile])
            return normalize_short(stack_half(rows[unit // HALVES], half), EPSILON)

        def emit(unit, features):
            tile, half = tiles[unit // HALVES], unit % HALVES
            for k, a in enumerate(half_rows(half)):
                g, j = k // HALF_STEP, k % HALF_STEP
                row = features[g * C : (g + 1) * C, j * LANES : (j + 1) * LANES]
                for part in range(2):
                    made[tile, a, part] = row[part * HALF : (part + 1) * HALF]

        stages = [
            lambda unit, _: load(unit),
            lambda unit, v: mm(first, v),
            lambda unit, v: gelu_scaled(v),
            lambda unit, v: normalize_short(v, EPSILON * (4.0 * SCALE * SCALE)),
            lambda unit, v: mm(second, v),
            lambda unit, v: gelu_scaled(v),
            lambda unit, v: normalize_short(v, EPSILON * (4.0 * SCALE * SCALE)),
            emit,
        ]
        units = PAIR * HALVES
        values = [None] * units
        for time in range(len(stages) + 2 * (units - 1)):
            for unit in range(units):
                stage = time - 2 * unit
                if 0 <= stage < len(stages):
                    values[unit] = stages[stage](unit, values[unit])
        for tile in tiles:
            copy = pltpu.make_async_copy(
                made.at[tile], gate_place(gate, tile), departures.at[tile]
            )
            copy.start()
        return carry

    lax.fori_loop(0, TILES // PAIR, body, 0)
    for t in range(TILES):
        pltpu.make_async_copy(made.at[t], gate_place(gate, t), departures.at[t]).wait()


def turn(weight):
    return weight[...].astype(F32).T


def pixel_kernel(
    picture, grid_bias,
    in_gain, in_weight, grid_gain, grid_wide, grid_gate_gain, grid_mixing, grid_narrow,
    block_gain, block_wide, out_weight,
    passed_out, kept_out, keys_out, total_out, final_weight, mixing_out,
    held, passed, kept, keys, total, arrivals, departures,
):
    fetch_tiles(picture, held, arrivals)

    place = lax.broadcasted_iota(jnp.int32, (CELLS, CELLS), 0)
    cell = lax.broadcasted_iota(jnp.int32, (CELLS, CELLS), 1)
    wanted = ((place // 32) * 2 + place % 2) * SIDE + (place // 2) % SIDE
    order = jnp.where(cell == wanted, 1.0, 0.0).astype(BF16)
    turned = mm_nt(order, grid_mixing[...]).astype(BF16)
    mixing_out[...] = mm_nt(turned, order).astype(BF16)

    out_turned = turn(out_weight)
    grid_both = mm_nt(out_turned[:, :C].astype(BF16), grid_narrow[...])
    final_weight[...] = fourfold(grid_both * (grid_gate_gain[...] * 8.0))
    grid_plain = fourfold(grid_both)
    out_grid, out_block = fourfold(out_turned[:, :C]), fourfold(out_turned[:, C:])
    first = turn(in_weight)
    first_grid, first_block = fourfold(first[:C]), fourfold(first[C:])
    grid_pass_weight = fourfold(turn(grid_wide)[:C])
    block_both = turn(block_wide)
    block_pass_weight, block_gate_weight = fourfold(block_both[:C]), fourfold(block_both[C:])
    in_rows, grid_rows = on_rows(in_gain[...]), on_rows(grid_gain[...])
    block_rows = on_rows(block_gain[...])
    own_cell = lax.axis_index("row") * 2 * SIDE + lax.axis_index("col")
    lane = lax.broadcasted_iota(jnp.int32, (1, CELLS), 1)

    def leaving(tile):
        pairs = [(passed, passed_out), (kept, kept_out), (keys, keys_out), (total, total_out)]
        return [
            pltpu.make_async_copy(made.at[tile], out.at[tile], departures.at[tile, k])
            for k, (made, out) in enumerate(pairs)
        ]

    def body(step, carry):
        tiles = [step * PAIR + k for k in range(PAIR)]
        for tile in tiles:
            wait_tile(picture, held, arrivals, tile)
        values = [pixels(held[tile]) for tile in tiles]
        normed = [normalize(v, in_rows) for v in values]
        grid_hidden = [gelu(mm(first_grid, v)) for v in normed]
        block_hidden = [gelu(mm(first_block, v)) for v in normed]
        normed = [normalize(v, block_rows) for v in block_hidden]
        features = [gelu(mm(block_gate_weight, v)) for v in normed]
        for tile, v in zip(tiles, normed):
            kept[tile] = gelu(mm(block_pass_weight, v))
        features = [normalize(v) for v in features]
        for tile, v in zip(tiles, features):
            for g in range(GROUPS):
                keys[tile, :, g * WIDE : (g + 1) * WIDE] = v[g * C : (g + 1) * C]
        normed = [normalize(v, grid_rows) for v in grid_hidden]
        grid_pass = [gelu(mm(grid_pass_weight, v)) for v in normed]
        for k, tile in enumerate(tiles):
            passed[tile] = grid_pass[k]
            cell = own_cell + tile // QUARTERS * SIDE
            own = jnp.sum(jnp.where(lane == cell, grid_bias[...], 0.0), axis=1, keepdims=True) + 1.0
            part = mm(out_grid, grid_hidden[k]) + mm(out_block, block_hidden[k])
            part = part + mm(grid_plain, (grid_pass[k].astype(F32) * own).astype(BF16))
            total[tile] = values[k].astype(F32) + part
        for tile in tiles:
            for copy in leaving(tile):
                copy.start()
        return carry

    lax.fori_loop(0, TILES // PAIR, body, 0)
    for t in range(TILES):
        for copy in leaving(t):
            copy.wait()


def block_kernel(
    token, passed_in, kept_in, keys_in, total_in,
    block_mixing, block_bias, block_gate_gain, block_narrow, out_weight,
    passed_head, base_head, base_out,
    spread, mixed, kept, keys, total, base, arrivals, departures,
):
    def coming(tile):
        pairs = [(keys_in, keys), (kept_in, kept), (total_in, total)]
        return [
            pltpu.make_async_copy(there.at[tile], here.at[tile], arrivals.at[tile, k])
            for k, (there, here) in enumerate(pairs)
        ]

    def head(tile):
        return pltpu.make_async_copy(
            passed_in.at[tile], passed_head.at[tile], arrivals.at[tile, 3]
        )

    def leaving(tile):
        return pltpu.make_async_copy(base.at[tile], base_out.at[tile], departures.at[tile])

    for t in range(TILES):
        for copy in coming(t):
            copy.start()
    for t in range(HEAD):
        head(t).start()

    source = lax.broadcasted_iota(jnp.int32, (CELLS, STRIP), 0)
    target = lax.broadcasted_iota(jnp.int32, (CELLS, STRIP), 1)
    chosen = (target // LANES) * SIDE + target % SIDE
    pick = jnp.where(source == chosen, 1.0, 0.0).astype(BF16)
    expanded = mm(block_mixing[...], pick).astype(BF16)
    same = lax.broadcasted_iota(jnp.int32, (LANES, STRIP), 0) // SIDE == (
        lax.broadcasted_iota(jnp.int32, (LANES, STRIP), 1) % LANES
    ) // SIDE
    mask = jnp.where(same, 1.0, 0.0).astype(BF16)
    for p in range(SIDE):
        rows = expanded[p * SIDE : (p + 1) * SIDE]
        rows = jnp.concatenate([rows] * (LANES // SIDE), axis=0)
        spread[p * LANES : (p + 1) * LANES, :] = rows * mask
    bias = block_bias[...]
    coarse = bias.astype(BF16)
    fine = (bias - coarse.astype(F32)).astype(BF16)
    offset = mm(coarse, pick) + mm(fine, pick) + 1.0
    offset = jnp.concatenate(
        [jnp.broadcast_to(offset[:, g * WIDE : (g + 1) * WIDE], (C, WIDE)) for g in range(GROUPS)],
        axis=0,
    )
    block_both = mm_nt(turn(out_weight)[:, C:].astype(BF16), block_narrow[...])
    block_gained = fourfold(block_both * block_gate_gain[...])
    block_plain = fourfold(block_both)

    for t in range(TILES):
        for copy in coming(t):
            copy.wait()
    for t in range(HEAD):
        head(t).wait()
    flat = keys[...].reshape(TILES * C, STRIP)

    def mix(step, carry):
        columns = pl.ds(pl.multiple_of(step * CELLS, CELLS), CELLS)
        mixed[:, columns] = mm(flat, spread[:, columns]).astype(BF16)
        return carry

    lax.fori_loop(0, STRIP // CELLS, mix, 0)

    def after(tile, carry):
        rows = pl.ds(pl.multiple_of(tile * C, C), C)
        blended = jnp.concatenate(
            [mixed[rows, g * WIDE : (g + 1) * WIDE] for g in range(GROUPS)], axis=0
        )
        through = kept[tile]
        part = mm(block_gained, through * blended)
        part = part + mm(block_plain, (through.astype(F32) * offset).astype(BF16))
        base[tile] = (total[tile] + part).astype(BF16)
        leaving(tile).start()
        return carry

    lax.fori_loop(0, TILES, after, 0)
    for t in range(TILES):
        leaving(t).wait()
    for t in range(HEAD):
        base_head[t] = base[t]


def sent_place(sent, cell, step, part):
    count = PEERS // MIX_PARTS
    return sent.at[pl.ds(part * count, count), cell, pl.ds(step * SIDE, SIDE), :]


def mix_kernel(arrived, mixing, sent, token, made, departures):
    weight = mixing[...]
    token[...] = jnp.zeros_like(token)
    count = PEERS // MIX_PARTS
    copies = []
    for step in range(HALF // SIDE):
        cells = arrived[:, :, pl.ds(step * SIDE, SIDE), :].reshape(CELLS, SIDE, LANES)
        cells = pltpu.einshape("kcl->ckl", cells)
        results = []
        for c in range(0, SIDE, 2):
            result = mm(weight, jnp.concatenate([cells[c], cells[c + 1]], axis=1)).astype(BF16)
            results += [result[:, :LANES], result[:, LANES:]]
        for part in range(MIX_PARTS):
            rows = slice(part * 2 * count, (part + 1) * 2 * count)
            mixed = pltpu.einshape("ckl->kcl", jnp.stack([r[rows] for r in results]))
            made[step, part] = mixed.reshape(count, 2, SIDE, LANES)
            for cell in range(2):
                copy = pltpu.make_async_copy(
                    made.at[step, part, :, cell],
                    sent_place(sent, cell, step, part),
                    departures.at[step, part, cell],
                )
                copy.start()
                copies.append(copy)
    for copy in copies:
        copy.wait()


def final_kernel(
    returned, passed_head, base_head, passed_in, base_in, weight,
    refined,
    passed, base, made, arrivals, departures,
):
    def coming(tile):
        return [
            pltpu.make_async_copy(passed_in.at[tile], passed.at[tile], arrivals.at[tile, 0]),
            pltpu.make_async_copy(base_in.at[tile], base.at[tile], arrivals.at[tile, 1]),
        ]

    for t in range(HEAD, TILES):
        for copy in coming(t):
            copy.start()
    final = weight[...]

    def blended(tile):
        cell = tile // QUARTERS
        quarter = tile % QUARTERS
        rows = pl.ds(pl.multiple_of(cell * HALF, HALF), HALF)
        return stack(
            [
                jnp.concatenate(
                    [returned[a, quarter, 0, rows, :], returned[a, quarter, 1, rows, :]], axis=0
                )
                for a in range(SIDE)
            ]
        )

    def finish(tiles, passed, base):
        values = [passed[tile] * blended(tile) for tile in tiles]
        values = [mm(final, v) for v in values]
        values = [(base[tile].astype(F32) + v).astype(BF16) for tile, v in zip(tiles, values)]
        for tile, v in zip(tiles, values):
            rows = jnp.stack([row_of(v, a) for a in range(SIDE)])
            made[tile] = pltpu.einshape("rcl->crl", rows)
        for tile in tiles:
            pltpu.make_async_copy(
                made.at[tile], refined.at[place_of(tile)], departures.at[tile]
            ).start()

    finish([jnp.int32(t) for t in range(HEAD)], passed_head, base_head)

    def body(step, carry):
        tiles = [HEAD + step * PAIR + k for k in range(PAIR)]
        for tile in tiles:
            for copy in coming(tile):
                copy.wait()
        finish(tiles, passed, base)
        return carry

    lax.fori_loop(0, (TILES - HEAD) // PAIR, body, 0)
    for t in range(TILES):
        pltpu.make_async_copy(made.at[t], refined.at[place_of(t)], departures.at[t]).wait()


VMEM, SMEM, HBM = pltpu.VMEM, pltpu.SMEM, pltpu.HBM


def kernel_call(kernel, name, places, outputs, scratch, limit, flops, *operands):
    operands = [
        pltpu.with_memory_space_constraint(value, place) if place in (HBM, VMEM) else value
        for value, place in zip(operands, places)
    ]
    return pl.pallas_call(
        kernel,
        in_specs=[pl.BlockSpec(memory_space=place or VMEM) for place in places],
        out_specs=[pl.BlockSpec(memory_space=place) for _, _, place in outputs],
        out_shape=[place(shape, kind) for shape, kind, place in outputs],
        scratch_shapes=scratch,
        name=name,
        cost_estimate=pl.CostEstimate(flops=flops, bytes_accessed=1 << 22, transcendentals=0),
        compiler_params=pltpu.CompilerParams(vmem_limit_bytes=limit << 20),
    )(*operands)


def exchange(values):
    pieces = values.reshape(PEERS, C, LANES)
    pieces = lax.all_to_all(pieces, ("row", "col"), split_axis=0, concat_axis=0, tiled=True)
    return pieces


GATE_SHAPE = (SIDE, QUARTERS, 2, C, LANES)
CELL_SHAPE = (PEERS, 2, HALF, LANES)
STACKED = (TILES, DEEP, WIDE)
KEYS = (TILES, C, STRIP)
BLOCKS = (TILES, C, SIDE, LANES)
DMA = pltpu.SemaphoreType.DMA


def gate_call(picture, in_gain, in_weight, wide_gain, wide_weight):
    return kernel_call(
        gate_kernel, "gate", [HBM] * 5, [(GATE_SHAPE, BF16, HBM)],
        [
            VMEM(BLOCKS, BF16),
            VMEM((TILES, SIDE, 2, HALF, LANES), BF16),
            VMEM((2, 1, C), F32),
            VMEM((2, C, 2 * C), BF16),
            DMA((TILES,)), DMA((TILES,)), DMA((4,)),
        ],
        24, 1 << 30, picture, in_gain, in_weight, wide_gain, wide_weight,
    )[0]


HEADS = (HEAD, DEEP, WIDE)


def pixel_call(*operands):
    return kernel_call(
        pixel_kernel, "pixel", [HBM] + [None] * 11,
        [
            (STACKED, BF16, HBM), (STACKED, BF16, HBM), (KEYS, BF16, HBM), (STACKED, F32, HBM),
            ((DEEP, DEEP), BF16, VMEM), ((CELLS, CELLS), BF16, VMEM),
        ],
        [
            VMEM(BLOCKS, BF16), VMEM(STACKED, BF16), VMEM(STACKED, BF16), VMEM(KEYS, BF16),
            VMEM(STACKED, F32), DMA((TILES,)), DMA((TILES, 4)),
        ],
        32, 20 << 30, *operands,
    )


def block_call(*operands):
    return kernel_call(
        block_kernel, "block", [VMEM] + [HBM] * 4 + [None] * 5,
        [(HEADS, BF16, VMEM), (HEADS, BF16, VMEM), (STACKED, BF16, HBM)],
        [
            VMEM((STRIP, STRIP), BF16), VMEM((TILES * C, STRIP), BF16), VMEM(STACKED, BF16),
            VMEM(KEYS, BF16), VMEM(STACKED, F32), VMEM(STACKED, BF16),
            DMA((TILES, 4)), DMA((TILES,)),
        ],
        40, 20 << 30, *operands,
    )


def mix_call(arrived, mixing):
    return kernel_call(
        mix_kernel, "mix", [VMEM, VMEM],
        [(CELL_SHAPE, BF16, HBM), ((8, LANES), F32, VMEM)],
        [
            VMEM((HALF // SIDE, MIX_PARTS, PEERS // MIX_PARTS, 2, SIDE, LANES), BF16),
            DMA((HALF // SIDE, MIX_PARTS, 2)),
        ],
        16, 1 << 30, arrived, mixing,
    )


def final_call(returned, passed_head, base_head, passed, base, weight, shape):
    return kernel_call(
        final_kernel, "final", [VMEM, VMEM, VMEM, HBM, HBM, VMEM], [(shape, BF16, HBM)],
        [
            VMEM(STACKED, BF16), VMEM(STACKED, BF16), VMEM(BLOCKS, BF16),
            DMA((TILES, 2)), DMA((TILES,)),
        ],
        24, 1 << 30, returned, passed_head, base_head, passed, base, weight,
    )[0]


def on_device(
    picture,
    input_gain,
    input_weight,
    grid_branch_scale,
    grid_widen_weight,
    grid_gate_scale,
    grid_mixing,
    grid_bias,
    grid_narrow_weight,
    block_branch_scale,
    block_widen_weight,
    block_gate_scale,
    block_mixing,
    block_bias,
    block_narrow_weight,
    output_weight,
):
    row = lambda gain: gain.reshape(1, -1)
    gate = gate_call(
        picture, row(input_gain), input_weight, row(grid_branch_scale), grid_widen_weight
    )
    arrived = exchange(gate).reshape(CELL_SHAPE)
    passed, kept, keys, total, final_weight, mixing = pixel_call(
        picture, row(grid_bias),
        row(input_gain), input_weight,
        row(grid_branch_scale), grid_widen_weight, row(grid_gate_scale), grid_mixing,
        grid_narrow_weight,
        row(block_branch_scale), block_widen_weight, output_weight,
    )
    sent, token = mix_call(arrived, mixing)
    returned = exchange(sent).reshape(GATE_SHAPE)
    passed_head, base_head, base = block_call(
        token, passed, kept, keys, total, block_mixing, row(block_bias), row(block_gate_scale),
        block_narrow_weight, output_weight,
    )
    return final_call(
        returned, passed_head, base_head, passed, base, final_weight, picture.shape
    )


def solution(mesh):
    return jax.shard_map(
        on_device,
        mesh=mesh,
        in_specs=(P(None, "row", "col"),) + (P(),) * 15,
        out_specs=P(None, "row", "col"),
        check_vma=False,
    )
```

```python
import jax
import jax.numpy as jnp
from jax import lax
from jax.experimental import pallas as pl
from jax.experimental.pallas import tpu as pltpu
from jax.sharding import PartitionSpec as P

F32 = jnp.float32
BF16 = jnp.bfloat16
C = 64
SIDE = 16
CELLS = 256
LANES = 128
COLS = 512
QUARTERS = COLS // LANES
TILES = 2 * QUARTERS
STRIP = SIDE * LANES
PEERS = 128
PAIR = 2
HALF = C // 2
GROUPS = 4
DEEP = GROUPS * C
WIDE = STRIP // GROUPS
EPSILON = 1e-06
GELU_A = 0.7978845608
GELU_B = 0.7978845608 * 0.044715
SCALE = GELU_B ** (1 / 3)
BEND = GELU_A / SCALE
HEAD = 2
MIX_PARTS = 2
HALVES = 2
HALF_STEP = SIDE // GROUPS // HALVES


def mm(a, b):
    return jnp.dot(a, b, preferred_element_type=F32)


def mm_nt(a, b):
    return lax.dot_general(a, b, (((1,), (1,)), ((), ())), preferred_element_type=F32)


def short(value):
    return jnp.array(value, BF16)


def normalize(values, gain=None):
    n = values.shape[1]
    values = values.astype(F32).reshape(GROUPS, C, n)
    centered = values - jnp.sum(values, axis=1, keepdims=True) * (1.0 / C)
    spread = jnp.sum(centered * centered, axis=1, keepdims=True) * (1.0 / C)
    centered = centered * lax.rsqrt(spread + EPSILON)
    if gain is not None:
        centered = centered * gain[None]
    return centered.astype(BF16).reshape(DEEP, n)


def gelu(values):
    bend = jnp.tanh(values * (GELU_B * (values * values) + GELU_A))
    half = 0.5 * values
    return (half * bend + half).astype(BF16)


def gelu_scaled(values):
    u = values.astype(BF16)
    return u * jnp.tanh(u * (u * u + short(BEND))) + u


def channel_sums(values):
    quads = (values[:, 0] + values[:, 1]) + (values[:, 2] + values[:, 3])
    return jnp.sum(quads.astype(F32), axis=1, keepdims=True)


def normalize_short(values, epsilon):
    n = values.shape[1]
    values = values.reshape(GROUPS, C // SIDE, SIDE, n)
    mean = jnp.broadcast_to(channel_sums(values) * (1.0 / C), (GROUPS, SIDE, n))
    high = mean.astype(BF16)
    low = (mean - high.astype(F32)).astype(BF16)
    centered = (values - high[:, None]) - low[:, None]
    factor = lax.rsqrt(channel_sums(centered * centered) + C * epsilon)
    factor = jnp.broadcast_to(factor, (GROUPS, SIDE, n)).astype(BF16)
    return (centered * factor[:, None]).reshape(DEEP, n)


def centered_weight(weight, gain):
    weight = weight * (gain * (8.0 * SCALE))
    return fourfold(weight - jnp.sum(weight, axis=1, keepdims=True) * (1.0 / C))


def fourfold(weight):
    wide = jnp.concatenate([weight.astype(BF16)] * GROUPS, axis=1)
    wide = jnp.concatenate([wide] * GROUPS, axis=0)
    rows = lax.broadcasted_iota(jnp.int32, (DEEP, DEEP), 0) // C
    columns = lax.broadcasted_iota(jnp.int32, (DEEP, DEEP), 1) // C
    return wide * jnp.where(rows == columns, 1.0, 0.0).astype(BF16)


def on_rows(gain):
    block = jnp.broadcast_to(gain, (LANES, C)).T
    return jnp.concatenate([block] * (WIDE // LANES), axis=1)


def place_of(tile):
    rows = pl.ds(pl.multiple_of(tile // QUARTERS * SIDE, SIDE), SIDE)
    lanes = pl.ds(pl.multiple_of(tile % QUARTERS * LANES, LANES), LANES)
    return slice(None), rows, lanes


def stack(rows):
    step = SIDE // GROUPS
    groups = [
        jnp.concatenate([rows[g * step + j] for j in range(step)], axis=1) for g in range(GROUPS)
    ]
    return jnp.concatenate(groups, axis=0)


def half_rows(half):
    step = SIDE // GROUPS
    return [g * step + half * HALF_STEP + j for g in range(GROUPS) for j in range(HALF_STEP)]


def stack_half(rows, half):
    chosen = [rows[a] for a in half_rows(half)]
    groups = [
        jnp.concatenate(chosen[g * HALF_STEP : (g + 1) * HALF_STEP], axis=1)
        for g in range(GROUPS)
    ]
    return jnp.concatenate(groups, axis=0)


def row_of(values, r):
    step = SIDE // GROUPS
    g, j = r // step, r % step
    return values[g * C : (g + 1) * C, j * LANES : (j + 1) * LANES]


def pixels(block):
    return stack(pltpu.einshape("crl->rcl", block))


def fetch_tiles(picture, held, arrivals):
    copies = [
        pltpu.make_async_copy(picture.at[place_of(t)], held.at[t], arrivals.at[t])
        for t in range(TILES)
    ]
    for copy in copies:
        copy.start()


def wait_tile(picture, held, arrivals, tile):
    pltpu.make_async_copy(picture.at[place_of(tile)], held.at[tile], arrivals.at[tile]).wait()


def gate_place(gate, tile):
    cell, quarter = tile // QUARTERS, tile % QUARTERS
    return gate.at[:, quarter, :, pl.ds(pl.multiple_of(cell * HALF, HALF), HALF), :]


def gate_kernel(
    picture, in_gain, in_weight, wide_gain, wide_weight,
    gate,
    held, made, gains, weights, arrivals, departures, small,
):
    parts = [
        pltpu.make_async_copy(in_weight, weights.at[0], small.at[0]),
        pltpu.make_async_copy(wide_weight, weights.at[1], small.at[1]),
        pltpu.make_async_copy(in_gain, gains.at[0], small.at[2]),
        pltpu.make_async_copy(wide_gain, gains.at[1], small.at[3]),
    ]
    for copy in parts:
        copy.start()
    fetch_tiles(picture, held, arrivals)
    for copy in parts:
        copy.wait()
    first = centered_weight(weights[0].astype(F32).T[:C], gains[0])
    second = centered_weight(weights[1].astype(F32).T[C:], gains[1])

    def body(step, carry):
        tiles = [step * PAIR + k for k in range(PAIR)]
        for tile in tiles:
            wait_tile(picture, held, arrivals, tile)
        rows = {}

        def load(unit):
            tile, half = tiles[unit // HALVES], unit % HALVES
            if half == 0:
                rows[unit // HALVES] = pltpu.einshape("crl->rcl", held[tile])
            return normalize_short(stack_half(rows[unit // HALVES], half), EPSILON)

        def emit(unit, features):
            tile, half = tiles[unit // HALVES], unit % HALVES
            for k, a in enumerate(half_rows(half)):
                g, j = k // HALF_STEP, k % HALF_STEP
                row = features[g * C : (g + 1) * C, j * LANES : (j + 1) * LANES]
                for part in range(2):
                    made[tile, a, part] = row[part * HALF : (part + 1) * HALF]

        stages = [
            lambda unit, _: load(unit),
            lambda unit, v: mm(first, v),
            lambda unit, v: gelu_scaled(v),
            lambda unit, v: normalize_short(v, EPSILON * (4.0 * SCALE * SCALE)),
            lambda unit, v: mm(second, v),
            lambda unit, v: gelu_scaled(v),
            lambda unit, v: normalize_short(v, EPSILON * (4.0 * SCALE * SCALE)),
            emit,
        ]
        units = PAIR * HALVES
        values = [None] * units
        for time in range(len(stages) + 2 * (units - 1)):
            for unit in range(units):
                stage = time - 2 * unit
                if 0 <= stage < len(stages):
                    values[unit] = stages[stage](unit, values[unit])
        for tile in tiles:
            copy = pltpu.make_async_copy(
                made.at[tile], gate_place(gate, tile), departures.at[tile]
            )
            copy.start()
        return carry

    lax.fori_loop(0, TILES // PAIR, body, 0)
    for t in range(TILES):
        pltpu.make_async_copy(made.at[t], gate_place(gate, t), departures.at[t]).wait()


def turn(weight):
    return weight[...].astype(F32).T


def pixel_kernel(
    picture, grid_bias,
    in_gain, in_weight, grid_gain, grid_wide, grid_gate_gain, grid_mixing, grid_narrow,
    block_gain, block_wide, out_weight,
    passed_out, kept_out, keys_out, total_out, final_weight, mixing_out,
    held, passed, kept, keys, total, arrivals, departures,
):
    fetch_tiles(picture, held, arrivals)

    place = lax.broadcasted_iota(jnp.int32, (CELLS, CELLS), 0)
    cell = lax.broadcasted_iota(jnp.int32, (CELLS, CELLS), 1)
    wanted = ((place // 32) * 2 + place % 2) * SIDE + (place // 2) % SIDE
    order = jnp.where(cell == wanted, 1.0, 0.0).astype(BF16)
    turned = mm_nt(order, grid_mixing[...]).astype(BF16)
    mixing_out[...] = mm_nt(turned, order).astype(BF16)

    out_turned = turn(out_weight)
    grid_both = mm_nt(out_turned[:, :C].astype(BF16), grid_narrow[...])
    final_weight[...] = fourfold(grid_both * (grid_gate_gain[...] * 8.0))
    grid_plain = fourfold(grid_both)
    out_grid, out_block = fourfold(out_turned[:, :C]), fourfold(out_turned[:, C:])
    first = turn(in_weight)
    first_grid, first_block = fourfold(first[:C]), fourfold(first[C:])
    grid_pass_weight = fourfold(turn(grid_wide)[:C])
    block_both = turn(block_wide)
    block_pass_weight, block_gate_weight = fourfold(block_both[:C]), fourfold(block_both[C:])
    in_rows, grid_rows = on_rows(in_gain[...]), on_rows(grid_gain[...])
    block_rows = on_rows(block_gain[...])
    own_cell = lax.axis_index("row") * 2 * SIDE + lax.axis_index("col")
    lane = lax.broadcasted_iota(jnp.int32, (1, CELLS), 1)

    def leaving(tile):
        pairs = [(passed, passed_out), (kept, kept_out), (keys, keys_out), (total, total_out)]
        return [
            pltpu.make_async_copy(made.at[tile], out.at[tile], departures.at[tile, k])
            for k, (made, out) in enumerate(pairs)
        ]

    def body(step, carry):
        tiles = [step * PAIR + k for k in range(PAIR)]
        for tile in tiles:
            wait_tile(picture, held, arrivals, tile)
        values = [pixels(held[tile]) for tile in tiles]
        normed = [normalize(v, in_rows) for v in values]
        grid_hidden = [gelu(mm(first_grid, v)) for v in normed]
        block_hidden = [gelu(mm(first_block, v)) for v in normed]
        normed = [normalize(v, block_rows) for v in block_hidden]
        features = [gelu(mm(block_gate_weight, v)) for v in normed]
        for tile, v in zip(tiles, normed):
            kept[tile] = gelu(mm(block_pass_weight, v))
        features = [normalize(v) for v in features]
        for tile, v in zip(tiles, features):
            for g in range(GROUPS):
                keys[tile, :, g * WIDE : (g + 1) * WIDE] = v[g * C : (g + 1) * C]
        normed = [normalize(v, grid_rows) for v in grid_hidden]
        grid_pass = [gelu(mm(grid_pass_weight, v)) for v in normed]
        for k, tile in enumerate(tiles):
            passed[tile] = grid_pass[k]
            cell = own_cell + tile // QUARTERS * SIDE
            own = jnp.sum(jnp.where(lane == cell, grid_bias[...], 0.0), axis=1, keepdims=True) + 1.0
            part = mm(out_grid, grid_hidden[k]) + mm(out_block, block_hidden[k])
            part = part + mm(grid_plain, (grid_pass[k].astype(F32) * own).astype(BF16))
            total[tile] = values[k].astype(F32) + part
        for tile in tiles:
            for copy in leaving(tile):
                copy.start()
        return carry

    lax.fori_loop(0, TILES // PAIR, body, 0)
    for t in range(TILES):
        for copy in leaving(t):
            copy.wait()


def block_kernel(
    token, passed_in, kept_in, keys_in, total_in,
    block_mixing, block_bias, block_gate_gain, block_narrow, out_weight,
    passed_head, base_head, base_out,
    spread, mixed, kept, keys, total, base, arrivals, departures,
):
    def coming(tile):
        pairs = [(keys_in, keys), (kept_in, kept), (total_in, total)]
        return [
            pltpu.make_async_copy(there.at[tile], here.at[tile], arrivals.at[tile, k])
            for k, (there, here) in enumerate(pairs)
        ]

    def head(tile):
        return pltpu.make_async_copy(
            passed_in.at[tile], passed_head.at[tile], arrivals.at[tile, 3]
        )

    def leaving(tile):
        return pltpu.make_async_copy(base.at[tile], base_out.at[tile], departures.at[tile])

    for t in range(TILES):
        for copy in coming(t):
            copy.start()
    for t in range(HEAD):
        head(t).start()

    source = lax.broadcasted_iota(jnp.int32, (CELLS, STRIP), 0)
    target = lax.broadcasted_iota(jnp.int32, (CELLS, STRIP), 1)
    chosen = (target // LANES) * SIDE + target % SIDE
    pick = jnp.where(source == chosen, 1.0, 0.0).astype(BF16)
    expanded = mm(block_mixing[...], pick).astype(BF16)
    same = lax.broadcasted_iota(jnp.int32, (LANES, STRIP), 0) // SIDE == (
        lax.broadcasted_iota(jnp.int32, (LANES, STRIP), 1) % LANES
    ) // SIDE
    mask = jnp.where(same, 1.0, 0.0).astype(BF16)
    for p in range(SIDE):
        rows = expanded[p * SIDE : (p + 1) * SIDE]
        rows = jnp.concatenate([rows] * (LANES // SIDE), axis=0)
        spread[p * LANES : (p + 1) * LANES, :] = rows * mask
    bias = block_bias[...]
    coarse = bias.astype(BF16)
    fine = (bias - coarse.astype(F32)).astype(BF16)
    offset = mm(coarse, pick) + mm(fine, pick) + 1.0
    offset = jnp.concatenate(
        [jnp.broadcast_to(offset[:, g * WIDE : (g + 1) * WIDE], (C, WIDE)) for g in range(GROUPS)],
        axis=0,
    )
    block_both = mm_nt(turn(out_weight)[:, C:].astype(BF16), block_narrow[...])
    block_gained = fourfold(block_both * block_gate_gain[...])
    block_plain = fourfold(block_both)

    for t in range(TILES):
        for copy in coming(t):
            copy.wait()
    for t in range(HEAD):
        head(t).wait()
    flat = keys[...].reshape(TILES * C, STRIP)

    def mix(step, carry):
        columns = pl.ds(pl.multiple_of(step * CELLS, CELLS), CELLS)
        mixed[:, columns] = mm(flat, spread[:, columns]).astype(BF16)
        return carry

    lax.fori_loop(0, STRIP // CELLS, mix, 0)

    def after(tile, carry):
        rows = pl.ds(pl.multiple_of(tile * C, C), C)
        blended = jnp.concatenate(
            [mixed[rows, g * WIDE : (g + 1) * WIDE] for g in range(GROUPS)], axis=0
        )
        through = kept[tile]
        part = mm(block_gained, through * blended)
        part = part + mm(block_plain, (through.astype(F32) * offset).astype(BF16))
        base[tile] = (total[tile] + part).astype(BF16)
        leaving(tile).start()
        return carry

    lax.fori_loop(0, TILES, after, 0)
    for t in range(TILES):
        leaving(t).wait()
    for t in range(HEAD):
        base_head[t] = base[t]


def sent_place(sent, cell, step, part):
    count = PEERS // MIX_PARTS
    return sent.at[pl.ds(part * count, count), cell, pl.ds(step * SIDE, SIDE), :]


def mix_kernel(arrived, mixing, sent, token, made, departures):
    weight = mixing[...]
    token[...] = jnp.zeros_like(token)
    count = PEERS // MIX_PARTS
    copies = []
    for step in range(HALF // SIDE):
        cells = arrived[:, :, pl.ds(step * SIDE, SIDE), :].reshape(CELLS, SIDE, LANES)
        cells = pltpu.einshape("kcl->ckl", cells)
        results = []
        for c in range(0, SIDE, 2):
            result = mm(weight, jnp.concatenate([cells[c], cells[c + 1]], axis=1)).astype(BF16)
            results += [result[:, :LANES], result[:, LANES:]]
        for part in range(MIX_PARTS):
            rows = slice(part * 2 * count, (part + 1) * 2 * count)
            mixed = pltpu.einshape("ckl->kcl", jnp.stack([r[rows] for r in results]))
            made[step, part] = mixed.reshape(count, 2, SIDE, LANES)
            for cell in range(2):
                copy = pltpu.make_async_copy(
                    made.at[step, part, :, cell],
                    sent_place(sent, cell, step, part),
                    departures.at[step, part, cell],
                )
                copy.start()
                copies.append(copy)
    for copy in copies:
        copy.wait()


def final_kernel(
    returned, passed_head, base_head, passed_in, base_in, weight,
    refined,
    passed, base, made, arrivals, departures,
):
    def coming(tile):
        return [
            pltpu.make_async_copy(passed_in.at[tile], passed.at[tile], arrivals.at[tile, 0]),
            pltpu.make_async_copy(base_in.at[tile], base.at[tile], arrivals.at[tile, 1]),
        ]

    for t in range(HEAD, TILES):
        for copy in coming(t):
            copy.start()
    final = weight[...]

    def blended(tile):
        cell = tile // QUARTERS
        quarter = tile % QUARTERS
        rows = pl.ds(pl.multiple_of(cell * HALF, HALF), HALF)
        return stack(
            [
                jnp.concatenate(
                    [returned[a, quarter, 0, rows, :], returned[a, quarter, 1, rows, :]], axis=0
                )
                for a in range(SIDE)
            ]
        )

    def finish(tiles, passed, base):
        values = [passed[tile] * blended(tile) for tile in tiles]
        values = [mm(final, v) for v in values]
        values = [(base[tile].astype(F32) + v).astype(BF16) for tile, v in zip(tiles, values)]
        for tile, v in zip(tiles, values):
            rows = jnp.stack([row_of(v, a) for a in range(SIDE)])
            made[tile] = pltpu.einshape("rcl->crl", rows)
            pltpu.make_async_copy(
                made.at[tile], refined.at[place_of(tile)], departures.at[tile]
            ).start()

    finish([jnp.int32(t) for t in range(HEAD)], passed_head, base_head)

    def body(step, carry):
        tiles = [HEAD + step * PAIR + k for k in range(PAIR)]
        for tile in tiles:
            for copy in coming(tile):
                copy.wait()
        finish(tiles, passed, base)
        return carry

    lax.fori_loop(0, (TILES - HEAD) // PAIR, body, 0)
    for t in range(TILES):
        pltpu.make_async_copy(made.at[t], refined.at[place_of(t)], departures.at[t]).wait()


VMEM, SMEM, HBM = pltpu.VMEM, pltpu.SMEM, pltpu.HBM


def kernel_call(kernel, name, places, outputs, scratch, limit, flops, *operands):
    operands = [
        pltpu.with_memory_space_constraint(value, place) if place in (HBM, VMEM) else value
        for value, place in zip(operands, places)
    ]
    return pl.pallas_call(
        kernel,
        in_specs=[pl.BlockSpec(memory_space=place or VMEM) for place in places],
        out_specs=[pl.BlockSpec(memory_space=place) for _, _, place in outputs],
        out_shape=[place(shape, kind) for shape, kind, place in outputs],
        scratch_shapes=scratch,
        name=name,
        cost_estimate=pl.CostEstimate(flops=flops, bytes_accessed=1 << 22, transcendentals=0),
        compiler_params=pltpu.CompilerParams(vmem_limit_bytes=limit << 20),
    )(*operands)


def exchange(values):
    pieces = values.reshape(PEERS, C, LANES)
    pieces = lax.all_to_all(pieces, ("row", "col"), split_axis=0, concat_axis=0, tiled=True)
    return pieces


GATE_SHAPE = (SIDE, QUARTERS, 2, C, LANES)
CELL_SHAPE = (PEERS, 2, HALF, LANES)
STACKED = (TILES, DEEP, WIDE)
KEYS = (TILES, C, STRIP)
BLOCKS = (TILES, C, SIDE, LANES)
DMA = pltpu.SemaphoreType.DMA


def gate_call(picture, in_gain, in_weight, wide_gain, wide_weight):
    return kernel_call(
        gate_kernel, "gate", [HBM] * 5, [(GATE_SHAPE, BF16, HBM)],
        [
            VMEM(BLOCKS, BF16),
            VMEM((TILES, SIDE, 2, HALF, LANES), BF16),
            VMEM((2, 1, C), F32),
            VMEM((2, C, 2 * C), BF16),
            DMA((TILES,)), DMA((TILES,)), DMA((4,)),
        ],
        24, 1 << 30, picture, in_gain, in_weight, wide_gain, wide_weight,
    )[0]


HEADS = (HEAD, DEEP, WIDE)


def pixel_call(*operands):
    return kernel_call(
        pixel_kernel, "pixel", [HBM] + [None] * 11,
        [
            (STACKED, BF16, HBM), (STACKED, BF16, HBM), (KEYS, BF16, HBM), (STACKED, F32, HBM),
            ((DEEP, DEEP), BF16, VMEM), ((CELLS, CELLS), BF16, VMEM),
        ],
        [
            VMEM(BLOCKS, BF16), VMEM(STACKED, BF16), VMEM(STACKED, BF16), VMEM(KEYS, BF16),
            VMEM(STACKED, F32), DMA((TILES,)), DMA((TILES, 4)),
        ],
        32, 20 << 30, *operands,
    )


def block_call(*operands):
    return kernel_call(
        block_kernel, "block", [VMEM] + [HBM] * 4 + [None] * 5,
        [(HEADS, BF16, VMEM), (HEADS, BF16, VMEM), (STACKED, BF16, HBM)],
        [
            VMEM((STRIP, STRIP), BF16), VMEM((TILES * C, STRIP), BF16), VMEM(STACKED, BF16),
            VMEM(KEYS, BF16), VMEM(STACKED, F32), VMEM(STACKED, BF16),
            DMA((TILES, 4)), DMA((TILES,)),
        ],
        40, 20 << 30, *operands,
    )


def mix_call(arrived, mixing):
    return kernel_call(
        mix_kernel, "mix", [VMEM, VMEM],
        [(CELL_SHAPE, BF16, HBM), ((8, LANES), F32, VMEM)],
        [
            VMEM((HALF // SIDE, MIX_PARTS, PEERS // MIX_PARTS, 2, SIDE, LANES), BF16),
            DMA((HALF // SIDE, MIX_PARTS, 2)),
        ],
        16, 1 << 30, arrived, mixing,
    )


def final_call(returned, passed_head, base_head, passed, base, weight, shape):
    return kernel_call(
        final_kernel, "final", [VMEM, VMEM, VMEM, HBM, HBM, VMEM], [(shape, BF16, HBM)],
        [
            VMEM(STACKED, BF16), VMEM(STACKED, BF16), VMEM(BLOCKS, BF16),
            DMA((TILES, 2)), DMA((TILES,)),
        ],
        24, 1 << 30, returned, passed_head, base_head, passed, base, weight,
    )[0]


def on_device(
    picture,
    input_gain,
    input_weight,
    grid_branch_scale,
    grid_widen_weight,
    grid_gate_scale,
    grid_mixing,
    grid_bias,
    grid_narrow_weight,
    block_branch_scale,
    block_widen_weight,
    block_gate_scale,
    block_mixing,
    block_bias,
    block_narrow_weight,
    output_weight,
):
    row = lambda gain: gain.reshape(1, -1)
    gate = gate_call(
        picture, row(input_gain), input_weight, row(grid_branch_scale), grid_widen_weight
    )
    arrived = exchange(gate).reshape(CELL_SHAPE)
    passed, kept, keys, total, final_weight, mixing = pixel_call(
        picture, row(grid_bias),
        row(input_gain), input_weight,
        row(grid_branch_scale), grid_widen_weight, row(grid_gate_scale), grid_mixing,
        grid_narrow_weight,
        row(block_branch_scale), block_widen_weight, output_weight,
    )
    sent, token = mix_call(arrived, mixing)
    returned = exchange(sent).reshape(GATE_SHAPE)
    passed_head, base_head, base = block_call(
        token, passed, kept, keys, total, block_mixing, row(block_bias), row(block_gate_scale),
        block_narrow_weight, output_weight,
    )
    return final_call(
        returned, passed_head, base_head, passed, base, final_weight, picture.shape
    )


def solution(mesh):
    return jax.shard_map(
        on_device,
        mesh=mesh,
        in_specs=(P(None, "row", "col"),) + (P(),) * 15,
        out_specs=P(None, "row", "col"),
        check_vma=False,
    )
```
